512 devices in a mesh: grp: 4 (over z_hi), dp: 8 (over z_lo, core), tp: 16 (over x, y).
Axes of the slice: x: 4, y: 4, z: 16 (z_hi: 4, z_lo: 4; z = z_hi * 4 + z_lo), core: 2. Of those that a mesh axis runs over, the one named last changes fastest.
Arguments:
- grad_partials: bfloat16 [8, 16384, 4096], P('dp', 'tp', 'grp'), may hold values from -6 to 6
- master: float32 [16384, 4096], P('tp', ('grp', 'dp')), may hold values from -0.046875 to 0.046875
- moment: float32 [16384, 4096], P('tp', ('grp', 'dp')), may hold values from -3 to 3
- second: float32 [16384, 4096], P('tp', ('grp', 'dp')), may hold values from 0.25 to 4
- state: bfloat16 [1024, 4096], P(('grp', 'dp'), 'tp'), may hold values from -6 to 6
- hidden: bfloat16 [4, 1024, 16384], P(None, ('grp', 'dp'), 'tp'), may hold values from -6 to 6
- queries: bfloat16 [4, 1024, 4096], P(None, ('grp', 'dp'), 'tp'), may hold values from -6 to 6
- fresh_kv: bfloat16 [4, 1024, 2, 512], P(None, ('grp', 'dp'), None, 'tp'), may hold values from -4 to 4
- cache_k: bfloat16 [1024, 128, 128], P(('grp', 'dp'), 'tp'), may hold values from -4 to 4
- cache_v: bfloat16 [1024, 128, 128], P(('grp', 'dp'), 'tp'), may hold values from -4 to 4
- cache_scale: bfloat16 [1024, 2, 128], P(('grp', 'dp'), None, 'tp'), may hold values from 0.25 to 256, as said below
- lengths: int32 [1024], P(('grp', 'dp')), may hold values from 16 to 128, as said below
Outputs:
- codes: bfloat16 [16384, 4096], P('tp', ('grp', 'dp'))
- state_out: bfloat16 [1024, 4096], P(('grp', 'dp'), 'tp')
The draws below stay inside these ranges and needn't reach their ends.
Inputs may be any that keep to these rules, and one draw needn't show every extreme that they name: `lengths`: 16 or more for every row; in every draw some row has exactly 16 and some row exactly 128. `cache_scale`: positive.
All inputs are finite; a program needn't handle non-finite values.
Results may differ from the reference program's by a relative error of at most 0.017.
Values may be sent and summed in bfloat16 or wider, within the bound.
No kernel may reach another device: no remote copies, remote signals or barrier semaphores. Data moves between devices by JAX's collectives and lax.ppermute only.
A program may use at most 64 MiB of HBM per device.

```python
import math
import jax
import jax.numpy as jnp
from jax import lax

D = 4096
FF = 16384
HD = 128
KVH = 4
BLK = 128
CACHE = 32
SINK = 4
STEPS = 4
QPG = 8
ROWS = 1024
N_DP = 8


def draw_lengths(key, part):
    key = jax.random.fold_in(key, 11)
    first, other = jax.random.split(key)
    base = jax.random.randint(first, (ROWS,), CACHE // 2, 4 * CACHE + 1)
    picks = jax.random.permutation(other, ROWS)
    base = base.at[picks[0]].set(4 * CACHE)
    base = base.at[picks[1]].set(CACHE // 2)
    return base.astype(jnp.int32)


def draw_cache_scale(key, part):
    key = jax.random.fold_in(key, 23)
    first = jax.random.fold_in(key, 0)
    shape = (ROWS, 2, KVH * CACHE)
    base = jnp.exp(jax.random.uniform(first, shape, jnp.float32, math.log(0.5), math.log(2.0)))
    return base.astype(jnp.bfloat16)


def spiked(result, key, source, target, parts, factor):
    def block_of(dim):
        return (jnp.arange(result.shape[dim]) // (result.shape[dim] // parts)).reshape((-1,) + (1,) * (result.ndim - 1 - dim))

    near = jax.random.permutation(key, parts)[block_of(target)]
    second = (block_of(target) + parts // 2) % parts
    return jnp.where((block_of(source) == near) | (block_of(source) == second), factor * result, result)


def block_levels(key, extent, shards, least, largest):
    level = 1.0
    for position, blocks in shards:
        steps = jax.random.uniform(jax.random.fold_in(jax.random.fold_in(key, 6), position), (blocks,), jnp.float32, least / len(shards), largest / len(shards))
        level = level * jnp.repeat(jnp.exp(steps), extent[position] // blocks).reshape((-1,) + (1,) * (len(extent) - 1 - position))
    return level


def centred(key, extent, scale, limit, pieces=(), held_as=jnp.bfloat16):
    drawn = jax.random.normal(key, extent, jnp.float32) * scale
    if len(pieces) > 0:
        drawn = block_levels(key, extent, pieces, -0.22, 0.18) * drawn
    return jnp.clip(drawn, min=-limit, max=limit).astype(held_as)


def gaussian_with(rng, extent, width, most, pieces, heavy, kind=jnp.bfloat16):
    entries = width * jax.random.normal(rng, extent, jnp.float32)
    if pieces:
        entries = entries * block_levels(rng, extent, pieces, -0.22, 0.18)
    return jnp.clip(spiked(entries, jax.random.fold_in(rng, 3), *heavy), -most, most).astype(kind)


def setup_inputs(seed: int = 0) -> dict:
    arg_keys = jax.random.split(jax.random.key(seed), 13)
    return {
        "grad_partials": gaussian_with(arg_keys[0], (N_DP, FF, D), 1.0, 6.0, ((0, 8), (1, 16), (2, 4)), (0, 2, 8, 2.0)),
        "master": centred(arg_keys[1], (FF, D), FF ** -0.5, 0.046875, ((0, 16), (1, 32)), jnp.float32),
        "moment": centred(arg_keys[2], (FF, D), 0.5, 3.0, ((0, 16), (1, 32)), jnp.float32),
        "second": jnp.clip(jnp.exp(math.log(4.0) - 2.7725887 * jax.random.uniform(arg_keys[3], (FF, D), jnp.float32) ** block_levels(arg_keys[3], (FF, D), ((0, 16), (1, 32)), -0.2, 0.2)), 0.25, 4.0),
        "state": centred(arg_keys[4], (ROWS, D), 1.0, 6.0, ((0, 32), (1, 16))),
        "hidden": centred(arg_keys[5], (STEPS, ROWS, FF), 1.0, 6.0, ((1, 32), (2, 16))),
        "queries": centred(arg_keys[6], (STEPS, ROWS, D), 1.0, 6.0, ((1, 32), (2, 16))),
        "fresh_kv": centred(arg_keys[7], (STEPS, ROWS, 2, KVH * HD), 1.0, 4.0, ((1, 32), (3, 16))),
        "cache_k": centred(arg_keys[8], (ROWS, KVH * CACHE, HD), 1.0, 4.0, ((0, 32), (1, 16))),
        "cache_v": centred(arg_keys[9], (ROWS, KVH * CACHE, HD), 1.0, 4.0, ((0, 32), (1, 16))),
        "cache_scale": draw_cache_scale(jax.random.fold_in(arg_keys[12], 71), 0),
        "lengths": draw_lengths(jax.random.fold_in(arg_keys[12], 71), 0),
    }


beta_first = 0.9
beta_second = 0.95
adam_eps = 1e-08
weight_decay = 0.1
learn_rate = 0.01
adam_count = 100.0
scale_eps = 1e-06

def adamw_update(master, moment, second, grad):
    moment_new = beta_first * moment + (1.0 - beta_first) * grad
    second_new = beta_second * second + (1.0 - beta_second) * grad * grad
    moment_hat = moment_new / (1.0 - beta_first ** adam_count)
    second_hat = second_new / (1.0 - beta_second ** adam_count)
    return master - learn_rate * (moment_hat / (jnp.sqrt(second_hat) + adam_eps) + weight_decay * master)

def quantize_blocks(weight, block):
    nrow, ncol = weight.shape
    tiles = weight.reshape(nrow // block, block, ncol // block, block)
    peak = lax.optimization_barrier(jnp.max(jnp.abs(tiles), axis=(1, 3)))
    scale = (peak + scale_eps).astype(jnp.bfloat16)
    codes = (tiles / scale.astype(jnp.float32)[:, None, :, None]).astype(jnp.bfloat16)
    return (codes.reshape(nrow, ncol), scale)

def slot_mask(lengths, step, cache_len, sink):
    window = cache_len - sink
    slots = jnp.arange(cache_len, dtype=jnp.int32)
    keep = slots[None, :] < lengths[:, None]
    for done in range(step + 1):
        evicted = sink + (lengths + done - sink) % window
        keep = keep & (slots[None, :] != evicted[:, None])
    return keep

def attend(query, cache_k, cache_v, cache_scale, keep, new_keys, new_values, step):
    nrow, groups, heads, head = query.shape
    inv = 1.0 / math.sqrt(head)
    seen = jnp.arange(new_keys.shape[2], dtype=jnp.int32) <= step
    qf = query.astype(jnp.float32)
    old = jnp.einsum('rgqh,rgjh->rgqj', qf, cache_k.astype(jnp.float32)) * (cache_scale[:, :, 0, None, :] * inv)
    old = jnp.where(keep[:, None, None, :], old, -jnp.inf)
    fresh = jnp.einsum('rgqh,rgsh->rgqs', qf, new_keys.astype(jnp.float32)) * inv
    fresh = jnp.where(seen[None, None, None, :], fresh, -jnp.inf)
    top = jnp.maximum(lax.optimization_barrier(jnp.max(old, axis=-1)), lax.optimization_barrier(jnp.max(fresh, axis=-1)))[..., None]
    old_w = jnp.exp(old - top)
    fresh_w = jnp.exp(fresh - top)
    total = lax.optimization_barrier(jnp.sum(old_w, axis=-1, keepdims=True)) + lax.optimization_barrier(jnp.sum(fresh_w, axis=-1, keepdims=True))
    old_p = (old_w / total * cache_scale[:, :, 1, None, :]).astype(jnp.bfloat16)
    fresh_p = (fresh_w / total).astype(jnp.bfloat16)
    out = jnp.einsum('rgqj,rgjh->rgqh', old_p.astype(jnp.float32), cache_v.astype(jnp.float32))
    out = out + jnp.einsum('rgqs,rgsh->rgqh', fresh_p.astype(jnp.float32), new_values.astype(jnp.float32))
    return out.reshape(nrow, groups * heads * head)

def project_hidden(rows_hidden, codes, scale_cols):
    nblock = codes.shape[0] // BLK

    def add_block(index, total):
        start = (index * BLK).astype(jnp.int32)
        piece = lax.dynamic_slice_in_dim(rows_hidden, start, BLK, 1)
        block = lax.dynamic_slice_in_dim(codes, start, BLK, 0)
        factor = lax.dynamic_slice_in_dim(scale_cols, index.astype(jnp.int32), 1, 0)
        return total + jnp.dot(piece, block, preferred_element_type=jnp.float32) * factor
    empty = jnp.zeros((rows_hidden.shape[0], codes.shape[1]), jnp.float32)
    return lax.fori_loop(0, nblock, add_block, empty)

def reference(grad_partials, master, moment, second, state, hidden, queries, fresh_kv, cache_k, cache_v, cache_scale, lengths):
    grad = grad_partials[0].astype(jnp.float32)
    for index in range(1, N_DP):
        grad = grad + grad_partials[index].astype(jnp.float32)
    weight = adamw_update(master, moment, second, grad)
    codes, scale = quantize_blocks(weight, BLK)
    scale_cols = jnp.repeat(scale.astype(jnp.float32), BLK, axis=1)
    nrow = state.shape[0]
    keys_all = cache_k.reshape(nrow, KVH, CACHE, HD)
    values_all = cache_v.reshape(nrow, KVH, CACHE, HD)
    scale_all = cache_scale.astype(jnp.float32).reshape(nrow, 2, KVH, CACHE).transpose(0, 2, 1, 3)
    fresh = fresh_kv.reshape(STEPS, nrow, 2, KVH, HD)
    new_keys = fresh[:, :, 0].transpose(1, 2, 0, 3)
    new_values = fresh[:, :, 1].transpose(1, 2, 0, 3)
    for step in range(STEPS):
        query = queries[step].reshape(nrow, KVH, QPG, HD)
        keep = slot_mask(lengths, step, CACHE, SINK)
        attention = attend(query, keys_all, values_all, scale_all, keep, new_keys, new_values, step)
        mixed = project_hidden(hidden[step], codes, scale_cols)
        state = (state.astype(jnp.float32) + attention + mixed).astype(jnp.bfloat16)
    return (codes, state)
```

```python
import math

import jax
import jax.numpy as jnp
import numpy as np
from jax import lax
from jax.experimental import pallas as pl
from jax.experimental.pallas import tpu as pltpu
from jax.sharding import PartitionSpec as P

HD = 128
BLK = 128
CACHE = 32
SINK = 4
STEPS = 4
QUADS = 4
CHIPS = 16
ROWS = 32
UNITS = 1024
SLOTS = CACHE // QUADS

beta_first = 0.9
beta_second = 0.95
adam_eps = 1e-08
weight_decay = 0.1
learn_rate = 0.01
adam_count = 100.0
scale_eps = 1e-06

Z = ("grp", "dp")
ALL = ("grp", "dp", "tp")
F32 = jnp.float32
BF16 = jnp.bfloat16
VMEM_LIMIT = 48 * 1024 * 1024


def params():
    return pltpu.CompilerParams(vmem_limit_bytes=VMEM_LIMIT)


def ring_distance(a, b, n):
    d = abs(a - b) % n
    return min(d, n - d)


def row_places():
    places = []
    for c in range(CHIPS):
        by_z = sorted(range(CHIPS), key=lambda r: (-ring_distance(c, r, CHIPS), r))
        by_xy = sorted(
            range(CHIPS),
            key=lambda p: (ring_distance(p // 4, c // 4, 4) + ring_distance(p % 4, c % 4, 4), p),
        )
        place = [0] * CHIPS
        for r, p in zip(by_z, by_xy):
            place[r] = p
        places.append(place)
    return places


PLACES = row_places()
ROW_AT = np.argsort(np.array(PLACES), axis=1).astype(np.int32)


def home_pairs():
    return [
        ((c * 2 + b) * CHIPS + PLACES[c][r], (r * 2 + b) * CHIPS + c)
        for c in range(CHIPS)
        for b in range(2)
        for r in range(CHIPS)
    ]


def flip(value, mask):
    return lax.ppermute(value, "dp", [(s, s ^ mask) for s in range(8)])


def split_kernel(index_ref, grad_ref, out_ref):
    out_ref[0] = grad_ref[...]


def take_chunks(index, grad):
    return pl.pallas_call(
        split_kernel,
        grid_spec=pltpu.PrefetchScalarGridSpec(
            num_scalar_prefetch=1,
            grid=(4,),
            in_specs=[pl.BlockSpec((UNITS, BLK), lambda j, index: (0, index[j]))],
            out_specs=pl.BlockSpec((1, UNITS, BLK), lambda j, index: (j, 0, 0)),
        ),
        out_shape=jax.ShapeDtypeStruct((4, UNITS, BLK), BF16),
        compiler_params=params(),
        name="take_chunks",
    )(index, grad)


def core_sum_kernel(index_ref, near_ref, far_ref, near_in_ref, far_in_ref, keep_ref, send_ref):
    keep_ref[0] = (near_ref[...].astype(F32) + near_in_ref[0].astype(F32)).astype(BF16)
    send_ref[0] = (far_ref[...].astype(F32) + far_in_ref[0].astype(F32)).astype(BF16)


def core_sum(index, grad, received):
    whole = lambda shift: pl.BlockSpec((UNITS, BLK), lambda j, index: (0, index[j + shift]))
    part = lambda shift: pl.BlockSpec((1, UNITS, BLK), lambda j, index: (j + shift, 0, 0))
    shape = jax.ShapeDtypeStruct((2, UNITS, BLK), BF16)
    return pl.pallas_call(
        core_sum_kernel,
        grid_spec=pltpu.PrefetchScalarGridSpec(
            num_scalar_prefetch=1,
            grid=(2,),
            in_specs=[whole(0), whole(2), part(0), part(2)],
            out_specs=[part(0), part(0)],
        ),
        out_shape=[shape, shape],
        compiler_params=params(),
        name="core_sum",
    )(index, grad, grad, received, received)


def pair_sum_kernel(keep_ref, received_ref, out_ref):
    out_ref[...] = (keep_ref[0].astype(F32) + received_ref[0].astype(F32)).astype(BF16)


def pair_sum(keep, received):
    spec = pl.BlockSpec((1, UNITS, BLK), lambda i: (1, 0, 0))
    return pl.pallas_call(
        pair_sum_kernel,
        grid=(1,),
        in_specs=[spec, spec],
        out_specs=pl.BlockSpec((UNITS, BLK), lambda i: (0, 0)),
        out_shape=jax.ShapeDtypeStruct((UNITS, BLK), BF16),
        compiler_params=params(),
        name="pair_sum",
    )(keep, received)


def update_kernel(
    keep_ref, second_in_ref, third_in_ref, master_ref, moment_ref, second_ref, codes_ref, packed_ref
):
    for block in range(UNITS // BLK):
        rows = slice(block * BLK, (block + 1) * BLK)
        grad = (
            keep_ref[0, rows].astype(F32)
            + second_in_ref[0, rows].astype(F32)
            + third_in_ref[rows].astype(F32)
        )
        master = master_ref[rows]
        moment_new = beta_first * moment_ref[rows] + (1.0 - beta_first) * grad
        second_new = beta_second * second_ref[rows] + (1.0 - beta_second) * grad * grad
        moment_hat = moment_new / (1.0 - beta_first**adam_count)
        second_hat = second_new / (1.0 - beta_second**adam_count)
        weight = master - learn_rate * (
            moment_hat / (jnp.sqrt(second_hat) + adam_eps) + weight_decay * master
        )
        peak = jnp.max(jnp.max(jnp.abs(weight), axis=0, keepdims=True), axis=1, keepdims=True)
        scale = (peak + scale_eps).astype(BF16)
        codes = (weight / scale.astype(F32)).astype(BF16)
        codes_ref[rows] = codes
        packed_ref[rows] = codes
        packed_ref[UNITS + 16 * block : UNITS + 16 * (block + 1)] = jnp.broadcast_to(
            scale, (16, BLK)
        )


PACKED = UNITS + 16 * (UNITS // BLK)


def update(keep, second_in, third_in, master, moment, second):
    first = pl.BlockSpec((1, UNITS, BLK), lambda i: (0, 0, 0))
    flat = pl.BlockSpec((UNITS, BLK), lambda i: (0, 0))
    return pl.pallas_call(
        update_kernel,
        grid=(1,),
        in_specs=[first, first, flat, flat, flat, flat],
        out_specs=[flat, pl.BlockSpec((PACKED, BLK), lambda i: (0, 0))],
        out_shape=[
            jax.ShapeDtypeStruct((UNITS, BLK), BF16),
            jax.ShapeDtypeStruct((PACKED, BLK), BF16),
        ],
        compiler_params=params(),
        name="update",
    )(keep, second_in, third_in, master, moment, second)


def project_kernel(order_ref, near_ref, far_ref, own_ref, other_ref, out_ref, sums):
    half = CHIPS // 2
    core = order_ref[CHIPS]
    for side, rows_ref in enumerate((near_ref, far_ref)):
        for which, codes_ref in enumerate((own_ref, other_ref)):
            total = jnp.zeros((half * ROWS, BLK), F32)
            for block in range(UNITS // BLK):
                rows = rows_ref[:, :, block * BLK : (block + 1) * BLK].reshape(half * ROWS, BLK)
                codes = codes_ref[block * BLK : (block + 1) * BLK]
                scale = codes_ref[UNITS + 16 * block : UNITS + 16 * (block + 1)][:1].astype(F32)
                total = total + jnp.dot(rows, codes, preferred_element_type=F32) * scale
            sums[which, side * half : (side + 1) * half] = total.astype(BF16).reshape(
                half, ROWS, BLK
            )
    for place in range(CHIPS):
        row_block = order_ref[place]
        out_ref[place, core] = sums[0, row_block]
        out_ref[place, 1 - core] = sums[1, row_block]


def project(order, near, far, own, other):
    return pl.pallas_call(
        project_kernel,
        grid_spec=pltpu.PrefetchScalarGridSpec(
            num_scalar_prefetch=1,
            grid=(1,),
            in_specs=[
                pl.BlockSpec((CHIPS // 2, ROWS, UNITS), lambda i, order: (0, 0, 0)),
                pl.BlockSpec((CHIPS // 2, ROWS, UNITS), lambda i, order: (0, 0, 0)),
                pl.BlockSpec((PACKED, BLK), lambda i, order: (0, 0)),
                pl.BlockSpec((PACKED, BLK), lambda i, order: (0, 0)),
            ],
            out_specs=pl.BlockSpec((CHIPS, 2, ROWS, BLK), lambda i, order: (0, 0, 0, 0)),
            scratch_shapes=[pltpu.VMEM((2, CHIPS, ROWS, BLK), BF16)],
        ),
        out_shape=jax.ShapeDtypeStruct((CHIPS, 2, ROWS, BLK), BF16),
        compiler_params=params(),
        name="project",
    )(order, near, far, own, other)


def unit_sum_kernel(parts_ref, out_ref):
    total = parts_ref[0].astype(F32)
    for index in range(1, CHIPS):
        total = total + parts_ref[index].astype(F32)
    out_ref[...] = total.astype(BF16)


def unit_sum(parts):
    return pl.pallas_call(
        unit_sum_kernel,
        out_shape=jax.ShapeDtypeStruct((2, ROWS, BLK), BF16),
        compiler_params=params(),
        name="unit_sum",
    )(parts)


def finish_kernel(state_ref, attention_ref, mixed_ref, out_ref):
    for half in range(2):
        cols = slice(half * BLK, (half + 1) * BLK)
        out_ref[:, cols] = (
            state_ref[:, cols].astype(F32) + attention_ref[:, cols] + mixed_ref[half].astype(F32)
        ).astype(BF16)


def finish(state, attention, mixed):
    return pl.pallas_call(
        finish_kernel,
        out_shape=jax.ShapeDtypeStruct(state.shape, BF16),
        compiler_params=params(),
        name="finish",
    )(state, attention, mixed)


KEYS = ROWS * SLOTS
FRESH = STEPS * ROWS
KV_ROWS = 2 * KEYS + 2 * FRESH + 16


def pack_caches(cache_k, cache_v, cache_scale, fresh_kv, place):
    width = fresh_kv.shape[3]
    fresh = fresh_kv.transpose(2, 0, 1, 3).reshape(2 * FRESH, width)
    lane = lax.broadcasted_iota(jnp.int32, (2 * FRESH, HD), 1)
    fresh = jnp.where(lane // width == place, jnp.tile(fresh, (1, HD // width)), 0)
    scale = cache_scale.transpose(1, 0, 2).reshape(2 * KEYS // HD, HD)
    scale = jnp.pad(scale, ((0, 16 - scale.shape[0]), (0, 0)))
    return jnp.concatenate(
        [cache_k.reshape(KEYS, HD), cache_v.reshape(KEYS, HD), fresh, scale], axis=0
    )


def attend_kernel(marks_ref, queries_ref, packed_ref, out_ref):
    inv = 1.0 / math.sqrt(HD)
    slots = QUADS * KEYS
    keys = packed_ref[:, :KEYS].reshape(slots, HD)
    values = packed_ref[:, KEYS : 2 * KEYS].reshape(slots, HD)
    fresh = packed_ref[0, 2 * KEYS : 2 * KEYS + 2 * FRESH].astype(F32)
    for place in range(1, QUADS):
        fresh = fresh + packed_ref[place, 2 * KEYS : 2 * KEYS + 2 * FRESH].astype(F32)
    fresh = fresh.astype(BF16)
    new_keys, new_values = fresh[:FRESH], fresh[FRESH:]
    scales = packed_ref[:, 2 * KEYS + 2 * FRESH :].astype(F32)
    lines = KEYS // HD
    key_scale = jnp.concatenate(
        [scales[p, i : i + 1] for p in range(QUADS) for i in range(lines)], axis=1
    )
    value_scale = jnp.concatenate(
        [scales[p, lines + i : lines + i + 1] for p in range(QUADS) for i in range(lines)], axis=1
    )
    lane = lax.broadcasted_iota(jnp.int32, (ROWS, slots), 1)
    row = lax.broadcasted_iota(jnp.int32, (ROWS, slots), 0)
    slot = (lane // KEYS) * SLOTS + (lane & (SLOTS - 1))
    live = ((lane // SLOTS) & (ROWS - 1)) == row
    live = live & (slot < marks_ref[:, 0:1])
    new_lane = lax.broadcasted_iota(jnp.int32, (ROWS, FRESH), 1)
    new_row = lax.broadcasted_iota(jnp.int32, (ROWS, FRESH), 0)
    mine = (new_lane & (ROWS - 1)) == new_row
    old_sum = [jnp.zeros((ROWS, slots), F32) for _ in range(2)]
    new_sum = [jnp.zeros((ROWS, FRESH), F32) for _ in range(2)]
    for step in range(STEPS):
        live = live & (slot != marks_ref[:, step + 1 : step + 2])
        seen = mine & (new_lane // ROWS <= step)
        for head in range(2):
            query = queries_ref[step, :, head * HD : (head + 1) * HD]
            across = (((1,), (1,)), ((), ()))
            old = lax.dot_general(query, keys, across, preferred_element_type=F32)
            old = jnp.where(live, old * (key_scale * inv), -jnp.inf)
            new = lax.dot_general(query, new_keys, across, preferred_element_type=F32) * inv
            new = jnp.where(seen, new, -jnp.inf)
            top = jnp.maximum(
                jnp.max(old, axis=1, keepdims=True), jnp.max(new, axis=1, keepdims=True)
            )
            old = jnp.exp(old - top)
            new = jnp.exp(new - top)
            share = 1.0 / (jnp.sum(old, axis=1, keepdims=True) + jnp.sum(new, axis=1, keepdims=True))
            old_sum[head] = old_sum[head] + old * share
            new_sum[head] = new_sum[head] + new * share
    for head in range(2):
        old = (old_sum[head] * value_scale).astype(BF16)
        new = new_sum[head].astype(BF16)
        out_ref[:, head * HD : (head + 1) * HD] = jnp.dot(
            old, values, preferred_element_type=F32
        ) + jnp.dot(new, new_values, preferred_element_type=F32)


def attend(lengths, queries, packed):
    steps = jnp.arange(STEPS, dtype=jnp.int32)
    evicted = SINK + (lengths[:, None] + steps[None, :] - SINK) % (CACHE - SINK)
    marks = jnp.concatenate(
        [lengths[:, None], evicted, jnp.zeros((ROWS, HD - 1 - STEPS), jnp.int32)], axis=1
    )
    return pl.pallas_call(
        attend_kernel,
        out_shape=jax.ShapeDtypeStruct((ROWS, 2 * HD), F32),
        compiler_params=params(),
        name="attend",
    )(marks, queries, packed)


def shards(
    grad_partials,
    master,
    moment,
    second,
    state,
    hidden,
    queries,
    fresh_kv,
    cache_k,
    cache_v,
    cache_scale,
    lengths,
):
    dp = lax.axis_index("dp")
    tp = lax.axis_index("tp")
    core, low = dp % 2, dp // 2
    plane = lax.axis_index("grp") * 4 + low
    grad = grad_partials[0]

    owners = low ^ jnp.array([0, 2, 1, 3], jnp.int32)
    outgoing = take_chunks(2 * owners + 1 - core, grad)
    units = jnp.sum(hidden.astype(F32), axis=0).astype(BF16)
    received = flip(outgoing, 1)
    keep, send = core_sum(2 * owners + core, grad, received)
    second_in = flip(send, 2)

    units, send = lax.optimization_barrier((units, send))
    parity_groups = [
        [g * 8 + (2 * h + l) * 2 + b for g in range(4) for h in range(2)]
        for l in range(2)
        for b in range(2)
    ]
    near = lax.all_gather(units, Z, axis=0, axis_index_groups=parity_groups)

    third = pair_sum(keep, second_in)
    third_in = flip(third, 4)
    far = flip(near, 2)

    caches = pack_caches(cache_k, cache_v, cache_scale, fresh_kv, tp % QUADS)
    caches, _ = lax.optimization_barrier((caches, third))
    quads = [[QUADS * x + y for y in range(QUADS)] for x in range(QUADS)]
    packed = lax.all_gather(caches, "tp", axis=0, axis_index_groups=quads)
    attention = attend(lengths, queries, packed)

    codes, own = update(keep, second_in, third_in, master, moment, second)
    other = flip(own, 1)

    row_at = lax.dynamic_index_in_dim(jnp.array(ROW_AT), plane, 0, keepdims=False)
    order = ((row_at ^ low) & 1) * (CHIPS // 2) + row_at // 2
    order = jnp.concatenate([order, core[None]]).astype(jnp.int32)
    parts = project(order, near, far, own, other)
    parts = lax.all_to_all(parts, "tp", 0, 0)
    mixed = lax.ppermute(unit_sum(parts), ALL, home_pairs())
    return (codes, finish(state, attention, mixed))


def solution(mesh):
    return jax.shard_map(
        shards,
        mesh=mesh,
        in_specs=(
            P("dp", "tp", "grp"),
            P("tp", ("grp", "dp")),
            P("tp", ("grp", "dp")),
            P("tp", ("grp", "dp")),
            P(("grp", "dp"), "tp"),
            P(None, ("grp", "dp"), "tp"),
            P(None, ("grp", "dp"), "tp"),
            P(None, ("grp", "dp"), None, "tp"),
            P(("grp", "dp"), "tp", None),
            P(("grp", "dp"), "tp", None),
            P(("grp", "dp"), None, "tp"),
            P(("grp", "dp")),
        ),
        out_specs=(P("tp", ("grp", "dp")), P(("grp", "dp"), "tp")),
        check_vma=False,
    )
```

```python
import math

import jax
import jax.numpy as jnp
import numpy as np
from jax import lax
from jax.experimental import pallas as pl
from jax.experimental.pallas import tpu as pltpu
from jax.sharding import PartitionSpec as P

HD = 128
BLK = 128
CACHE = 32
SINK = 4
STEPS = 4
QUADS = 4
CHIPS = 16
ROWS = 32
UNITS = 1024
SLOTS = CACHE // QUADS

beta_first = 0.9
beta_second = 0.95
adam_eps = 1e-08
weight_decay = 0.1
learn_rate = 0.01
adam_count = 100.0
scale_eps = 1e-06

Z = ("grp", "dp")
ALL = ("grp", "dp", "tp")
F32 = jnp.float32
BF16 = jnp.bfloat16
VMEM_LIMIT = 48 * 1024 * 1024


def params():
    return pltpu.CompilerParams(vmem_limit_bytes=VMEM_LIMIT)


def ring_distance(a, b, n):
    d = abs(a - b) % n
    return min(d, n - d)


def row_places():
    places = []
    for c in range(CHIPS):
        by_z = sorted(range(CHIPS), key=lambda r: (-ring_distance(c, r, CHIPS), r))
        by_xy = sorted(
            range(CHIPS),
            key=lambda p: (ring_distance(p // 4, c // 4, 4) + ring_distance(p % 4, c % 4, 4), p),
        )
        place = [0] * CHIPS
        for r, p in zip(by_z, by_xy):
            place[r] = p
        places.append(place)
    return places


PLACES = row_places()
ROW_AT = np.argsort(np.array(PLACES), axis=1).astype(np.int32)


def home_pairs():
    return [
        ((c * 2 + b) * CHIPS + PLACES[c][r], (r * 2 + b) * CHIPS + c)
        for c in range(CHIPS)
        for b in range(2)
        for r in range(CHIPS)
    ]


def flip(value, mask):
    return lax.ppermute(value, "dp", [(s, s ^ mask) for s in range(8)])


def from_plane(value, ahead):
    count = 2 * CHIPS
    return lax.ppermute(value, Z, [((d + 2 * ahead) % count, d) for d in range(count)])


def split_kernel(index_ref, grad_ref, out_ref):
    out_ref[0] = grad_ref[...]


def take_chunks(index, grad):
    return pl.pallas_call(
        split_kernel,
        grid_spec=pltpu.PrefetchScalarGridSpec(
            num_scalar_prefetch=1,
            grid=(4,),
            in_specs=[pl.BlockSpec((UNITS, BLK), lambda j, index: (0, index[j]))],
            out_specs=pl.BlockSpec((1, UNITS, BLK), lambda j, index: (j, 0, 0)),
        ),
        out_shape=jax.ShapeDtypeStruct((4, UNITS, BLK), BF16),
        compiler_params=params(),
        name="take_chunks",
    )(index, grad)


def core_sum_kernel(index_ref, near_ref, far_ref, near_in_ref, far_in_ref, keep_ref, send_ref):
    keep_ref[0] = (near_ref[...].astype(F32) + near_in_ref[0].astype(F32)).astype(BF16)
    send_ref[0] = (far_ref[...].astype(F32) + far_in_ref[0].astype(F32)).astype(BF16)


def core_sum(index, grad, received):
    whole = lambda shift: pl.BlockSpec((UNITS, BLK), lambda j, index: (0, index[j + shift]))
    part = lambda shift: pl.BlockSpec((1, UNITS, BLK), lambda j, index: (j + shift, 0, 0))
    shape = jax.ShapeDtypeStruct((2, UNITS, BLK), BF16)
    return pl.pallas_call(
        core_sum_kernel,
        grid_spec=pltpu.PrefetchScalarGridSpec(
            num_scalar_prefetch=1,
            grid=(2,),
            in_specs=[whole(0), whole(2), part(0), part(2)],
            out_specs=[part(0), part(0)],
        ),
        out_shape=[shape, shape],
        compiler_params=params(),
        name="core_sum",
    )(index, grad, grad, received, received)


def pair_sum_kernel(keep_ref, received_ref, out_ref):
    out_ref[...] = (keep_ref[0].astype(F32) + received_ref[0].astype(F32)).astype(BF16)


def pair_sum(keep, received):
    spec = pl.BlockSpec((1, UNITS, BLK), lambda i: (1, 0, 0))
    return pl.pallas_call(
        pair_sum_kernel,
        grid=(1,),
        in_specs=[spec, spec],
        out_specs=pl.BlockSpec((UNITS, BLK), lambda i: (0, 0)),
        out_shape=jax.ShapeDtypeStruct((UNITS, BLK), BF16),
        compiler_params=params(),
        cost_estimate=pl.CostEstimate(flops=10**11, bytes_accessed=10**9, transcendentals=0),
        name="pair_sum",
    )(keep, received)


def update_kernel(
    keep_ref, second_in_ref, third_in_ref, master_ref, moment_ref, second_ref, codes_ref, packed_ref
):
    for block in range(UNITS // BLK):
        rows = slice(block * BLK, (block + 1) * BLK)
        grad = (
            keep_ref[0, rows].astype(F32)
            + second_in_ref[0, rows].astype(F32)
            + third_in_ref[rows].astype(F32)
        )
        master = master_ref[rows]
        moment_new = beta_first * moment_ref[rows] + (1.0 - beta_first) * grad
        second_new = beta_second * second_ref[rows] + (1.0 - beta_second) * grad * grad
        moment_hat = moment_new / (1.0 - beta_first**adam_count)
        second_hat = second_new / (1.0 - beta_second**adam_count)
        weight = master - learn_rate * (
            moment_hat / (jnp.sqrt(second_hat) + adam_eps) + weight_decay * master
        )
        peak = jnp.max(jnp.max(jnp.abs(weight), axis=0, keepdims=True), axis=1, keepdims=True)
        scale = (peak + scale_eps).astype(BF16)
        codes = (weight / scale.astype(F32)).astype(BF16)
        codes_ref[rows] = codes
        packed_ref[rows] = codes
        packed_ref[UNITS + 16 * block : UNITS + 16 * (block + 1)] = jnp.broadcast_to(
            scale, (16, BLK)
        )


PACKED = UNITS + 16 * (UNITS // BLK)


def update(keep, second_in, third_in, master, moment, second):
    first = pl.BlockSpec((1, UNITS, BLK), lambda i: (0, 0, 0))
    flat = pl.BlockSpec((UNITS, BLK), lambda i: (0, 0))
    return pl.pallas_call(
        update_kernel,
        grid=(1,),
        in_specs=[first, first, flat, flat, flat, flat],
        out_specs=[flat, pl.BlockSpec((PACKED, BLK), lambda i: (0, 0))],
        out_shape=[
            jax.ShapeDtypeStruct((UNITS, BLK), BF16),
            jax.ShapeDtypeStruct((PACKED, BLK), BF16),
        ],
        compiler_params=params(),
        name="update",
    )(keep, second_in, third_in, master, moment, second)


def project_kernel(order_ref, same_ref, up_ref, two_low_ref, two_high_ref, down_ref, own_ref, other_ref, out_ref, sums):
    core = order_ref[CHIPS]
    start = 0
    for rows_ref in (same_ref, up_ref, two_low_ref, two_high_ref, down_ref):
        count = rows_ref.shape[0]
        for which, codes_ref in enumerate((own_ref, other_ref)):
            total = jnp.zeros((count * ROWS, BLK), F32)
            for block in range(UNITS // BLK):
                rows = rows_ref[:, :, block * BLK : (block + 1) * BLK].reshape(count * ROWS, BLK)
                codes = codes_ref[block * BLK : (block + 1) * BLK]
                scale = codes_ref[UNITS + 16 * block : UNITS + 16 * (block + 1)][:1].astype(F32)
                total = total + jnp.dot(rows, codes, preferred_element_type=F32) * scale
            sums[which, start : start + count] = total.astype(BF16).reshape(count, ROWS, BLK)
        start += count
    for place in range(CHIPS):
        row_block = order_ref[place]
        out_ref[place, core] = sums[0, row_block]
        out_ref[place, 1 - core] = sums[1, row_block]


def project(order, row_sets, own, other):
    rows = lambda x: pl.BlockSpec(x.shape, lambda i, order: (0, 0, 0))
    packed = pl.BlockSpec((PACKED, BLK), lambda i, order: (0, 0))
    return pl.pallas_call(
        project_kernel,
        grid_spec=pltpu.PrefetchScalarGridSpec(
            num_scalar_prefetch=1,
            grid=(1,),
            in_specs=[rows(x) for x in row_sets] + [packed, packed],
            out_specs=pl.BlockSpec((CHIPS, 2, ROWS, BLK), lambda i, order: (0, 0, 0, 0)),
            scratch_shapes=[pltpu.VMEM((2, CHIPS, ROWS, BLK), BF16)],
        ),
        out_shape=jax.ShapeDtypeStruct((CHIPS, 2, ROWS, BLK), BF16),
        compiler_params=params(),
        name="project",
    )(order, *[pltpu.with_memory_space_constraint(x, pltpu.HBM) for x in row_sets], own, other)


def unit_sum_kernel(parts_ref, out_ref):
    total = parts_ref[0].astype(F32)
    for index in range(1, CHIPS):
        total = total + parts_ref[index].astype(F32)
    out_ref[...] = total.astype(BF16)


def unit_sum(parts):
    return pl.pallas_call(
        unit_sum_kernel,
        out_shape=jax.ShapeDtypeStruct((2, ROWS, BLK), BF16),
        compiler_params=params(),
        name="unit_sum",
    )(parts)


def finish_kernel(state_ref, attention_ref, mixed_ref, out_ref):
    for half in range(2):
        cols = slice(half * BLK, (half + 1) * BLK)
        out_ref[:, cols] = (
            state_ref[:, cols].astype(F32) + attention_ref[:, cols] + mixed_ref[half].astype(F32)
        ).astype(BF16)


def finish(state, attention, mixed):
    return pl.pallas_call(
        finish_kernel,
        out_shape=jax.ShapeDtypeStruct(state.shape, BF16),
        compiler_params=params(),
        name="finish",
    )(state, attention, mixed)


KEYS = ROWS * SLOTS
FRESH = 2 * STEPS * ROWS
SCALES_AT = 2 * KEYS + FRESH
CACHE_ROWS = SCALES_AT + 16


def pack_kernel(place_ref, keys_ref, values_ref, scale_ref, fresh_ref, out_ref):
    out_ref[:KEYS] = keys_ref[...]
    out_ref[KEYS : 2 * KEYS] = values_ref[...]
    width = fresh_ref.shape[1]
    wide = jnp.concatenate([fresh_ref[...].astype(F32)] * (HD // width), axis=1)
    lane = lax.broadcasted_iota(jnp.int32, wide.shape, 1)
    out_ref[2 * KEYS : SCALES_AT] = jnp.where(lane // width == place_ref[0], wide, 0.0).astype(BF16)
    spread = lax.broadcasted_iota(jnp.int32, (ROWS, KEYS), 1) // SLOTS
    spread = (spread == lax.broadcasted_iota(jnp.int32, (ROWS, KEYS), 0)).astype(BF16)
    lines = jnp.dot(scale_ref[...], spread, preferred_element_type=F32)
    slot = lax.broadcasted_iota(jnp.int32, lines.shape, 0) & (SLOTS - 1)
    lane = lax.broadcasted_iota(jnp.int32, lines.shape, 1) & (SLOTS - 1)
    lines = jnp.where(slot == lane, lines, 0.0)
    rows = [
        jnp.sum(lines[k * SLOTS : (k + 1) * SLOTS, i * HD : (i + 1) * HD], axis=0, keepdims=True)
        for k in range(2)
        for i in range(KEYS // HD)
    ]
    out_ref[SCALES_AT:] = jnp.concatenate(
        rows + [jnp.zeros((16 - len(rows), HD), F32)], axis=0
    ).astype(BF16)


def pack_caches(cache_k, cache_v, cache_scale, fresh_kv, place):
    vmem = pl.BlockSpec(memory_space=pltpu.VMEM)
    return pl.pallas_call(
        pack_kernel,
        in_specs=[pl.BlockSpec(memory_space=pltpu.SMEM)] + [vmem] * 4,
        out_specs=vmem,
        out_shape=jax.ShapeDtypeStruct((CACHE_ROWS, HD), BF16),
        compiler_params=params(),
        name="pack_caches",
    )(
        place[None],
        cache_k.reshape(KEYS, HD),
        cache_v.reshape(KEYS, HD),
        cache_scale.transpose(1, 2, 0).reshape(2 * SLOTS, ROWS),
        fresh_kv.reshape(FRESH, fresh_kv.shape[3]),
    )


def attend_kernel(lengths_ref, queries_ref, packed_ref, out_ref):
    inv = 1.0 / math.sqrt(HD)
    slots = QUADS * KEYS
    keys = packed_ref[:, :KEYS].reshape(slots, HD)
    values = packed_ref[:, KEYS : 2 * KEYS].reshape(slots, HD)
    fresh = packed_ref[0, 2 * KEYS : SCALES_AT].astype(F32)
    for place in range(1, QUADS):
        fresh = fresh + packed_ref[place, 2 * KEYS : SCALES_AT].astype(F32)
    new_keys = fresh.astype(BF16)
    new_values = pltpu.roll(fresh, FRESH - 1, 0).astype(BF16)
    scales = packed_ref[:, SCALES_AT:].astype(F32)
    lines = KEYS // HD
    key_scale = jnp.concatenate(
        [scales[p, i : i + 1] for p in range(QUADS) for i in range(lines)], axis=1
    )
    value_scale = jnp.concatenate(
        [scales[p, lines + i : lines + i + 1] for p in range(QUADS) for i in range(lines)], axis=1
    )
    row = lax.broadcasted_iota(jnp.int32, (ROWS, ROWS), 0)
    column = lax.broadcasted_iota(jnp.int32, (ROWS, ROWS), 1)
    length = jnp.where(row == column, lengths_ref[...].astype(F32), 0.0)
    length = jnp.sum(length, axis=1, keepdims=True).astype(jnp.int32)
    lane = lax.broadcasted_iota(jnp.int32, (ROWS, slots), 1)
    row = lax.broadcasted_iota(jnp.int32, (ROWS, slots), 0)
    slot = (lane // KEYS) * SLOTS + (lane & (SLOTS - 1))
    live = ((lane // SLOTS) & (ROWS - 1)) == row
    live = live & (slot < length)
    ahead = slot - length
    window = CACHE - SINK
    lane = lax.broadcasted_iota(jnp.int32, (ROWS, FRESH), 1)
    row = lax.broadcasted_iota(jnp.int32, (ROWS, FRESH), 0)
    mine = (((lane // 2) & (ROWS - 1)) == row) & ((lane & 1) == 0)
    old_sum = [jnp.zeros((ROWS, slots), F32) for _ in range(2)]
    new_sum = [jnp.zeros((ROWS, FRESH), F32) for _ in range(2)]
    for step in range(STEPS):
        evicted = ahead == step
        for turn in range(1, (4 * CACHE + STEPS) // window + 1):
            evicted = evicted | (ahead == step - turn * window)
        live = live & jnp.logical_not(evicted & (slot >= SINK))
        seen = mine & (lane // (2 * ROWS) <= step)
        for head in range(2):
            query = queries_ref[step, :, head * HD : (head + 1) * HD]
            across = (((1,), (1,)), ((), ()))
            old = lax.dot_general(query, keys, across, preferred_element_type=F32)
            old = jnp.where(live, old * (key_scale * inv), -jnp.inf)
            new = lax.dot_general(query, new_keys, across, preferred_element_type=F32) * inv
            new = jnp.where(seen, new, -jnp.inf)
            top = jnp.maximum(
                jnp.max(old, axis=1, keepdims=True), jnp.max(new, axis=1, keepdims=True)
            )
            old = jnp.exp(old - top)
            new = jnp.exp(new - top)
            share = 1.0 / (jnp.sum(old, axis=1, keepdims=True) + jnp.sum(new, axis=1, keepdims=True))
            old_sum[head] = old_sum[head] + old * share
            new_sum[head] = new_sum[head] + new * share
    for head in range(2):
        old = (old_sum[head] * value_scale).astype(BF16)
        new = new_sum[head].astype(BF16)
        out_ref[:, head * HD : (head + 1) * HD] = jnp.dot(
            old, values, preferred_element_type=F32
        ) + jnp.dot(new, new_values, preferred_element_type=F32)


def attend(lengths, queries, packed):
    return pl.pallas_call(
        attend_kernel,
        out_shape=jax.ShapeDtypeStruct((ROWS, 2 * HD), F32),
        compiler_params=params(),
        name="attend",
    )(lengths[None], queries, packed)


def shards(
    grad_partials,
    master,
    moment,
    second,
    state,
    hidden,
    queries,
    fresh_kv,
    cache_k,
    cache_v,
    cache_scale,
    lengths,
):
    dp = lax.axis_index("dp")
    tp = lax.axis_index("tp")
    core, low = dp % 2, dp // 2
    plane = lax.axis_index("grp") * 4 + low
    grad = grad_partials[0]

    owners = low ^ jnp.array([0, 2, 1, 3], jnp.int32)
    outgoing = take_chunks(2 * owners + 1 - core, grad)
    received = flip(outgoing, 1)
    keep, send = core_sum(2 * owners + core, grad, received)
    second_in = flip(send, 2)

    hidden, _ = lax.optimization_barrier((hidden, send))
    units = jnp.sum(hidden.astype(F32), axis=0).astype(BF16)
    same = jnp.broadcast_to(units, (4,) + units.shape)
    same = lax.all_to_all(same, "grp", 0, 0)

    caches = pack_caches(cache_k, cache_v, cache_scale, fresh_kv, tp % QUADS)
    caches = jnp.broadcast_to(caches, (QUADS,) + caches.shape)
    caches, _ = lax.optimization_barrier((caches, send))
    quads = [[QUADS * x + y for y in range(QUADS)] for x in range(QUADS)]
    packed = lax.all_to_all(caches, "tp", 0, 0, axis_index_groups=quads)

    third = pair_sum(keep, second_in)
    third_in = flip(third, 4)
    same, _ = lax.optimization_barrier((same, third))
    up = from_plane(same, 1)
    down = from_plane(same, -1)
    two_low = from_plane(same[:2], 2)
    two_high = from_plane(same[2:], -2)
    attention = attend(lengths, queries, packed)

    third_in, up, down, two_low, two_high = lax.optimization_barrier(
        (third_in, up, down, two_low, two_high)
    )
    codes, own = update(keep, second_in, third_in, master, moment, second)
    other = flip(own, 1)

    row_at = lax.dynamic_index_in_dim(jnp.array(ROW_AT), plane, 0, keepdims=False)
    order = ((row_at - low) & 3) * 4 + row_at // 4
    order = jnp.concatenate([order, core[None]]).astype(jnp.int32)
    parts = project(order, (same, up, two_low, two_high, down), own, other)
    parts = lax.all_to_all(parts, "tp", 0, 0)
    mixed = lax.ppermute(unit_sum(parts), ALL, home_pairs())
    return (codes, finish(state, attention, mixed))


def solution(mesh):
    return jax.shard_map(
        shards,
        mesh=mesh,
        in_specs=(
            P("dp", "tp", "grp"),
            P("tp", ("grp", "dp")),
            P("tp", ("grp", "dp")),
            P("tp", ("grp", "dp")),
            P(("grp", "dp"), "tp"),
            P(None, ("grp", "dp"), "tp"),
            P(None, ("grp", "dp"), "tp"),
            P(None, ("grp", "dp"), None, "tp"),
            P(("grp", "dp"), "tp", None),
            P(("grp", "dp"), "tp", None),
            P(("grp", "dp"), None, "tp"),
            P(("grp", "dp")),
        ),
        out_specs=(P("tp", ("grp", "dp")), P(("grp", "dp"), "tp")),
        check_vma=False,
    )
```

```python
import math

import jax
import jax.numpy as jnp
import numpy as np
from jax import lax
from jax.experimental import pallas as pl
from jax.experimental.pallas import tpu as pltpu
from jax.sharding import PartitionSpec as P

HD = 128
BLK = 128
CACHE = 32
SINK = 4
STEPS = 4
QUADS = 4
CHIPS = 16
ROWS = 32
UNITS = 1024
SLOTS = CACHE // QUADS

beta_first = 0.9
beta_second = 0.95
adam_eps = 1e-08
weight_decay = 0.1
learn_rate = 0.01
adam_count = 100.0
scale_eps = 1e-06

Z = ("grp", "dp")
ALL = ("grp", "dp", "tp")
F32 = jnp.float32
BF16 = jnp.bfloat16
VMEM_LIMIT = 48 * 1024 * 1024


def params():
    return pltpu.CompilerParams(vmem_limit_bytes=VMEM_LIMIT)


def ring_distance(a, b, n):
    d = abs(a - b) % n
    return min(d, n - d)


def row_places():
    places = []
    for c in range(CHIPS):
        by_z = sorted(range(CHIPS), key=lambda r: (-ring_distance(c, r, CHIPS), r))
        by_xy = sorted(
            range(CHIPS),
            key=lambda p: (ring_distance(p // 4, c // 4, 4) + ring_distance(p % 4, c % 4, 4), p),
        )
        place = [0] * CHIPS
        for r, p in zip(by_z, by_xy):
            place[r] = p
        places.append(place)
    return places


PLACES = row_places()
ROW_AT = np.argsort(np.array(PLACES), axis=1).astype(np.int32)


def home_pairs():
    return [
        ((c * 2 + b) * CHIPS + PLACES[c][r], (r * 2 + b) * CHIPS + c)
        for c in range(CHIPS)
        for b in range(2)
        for r in range(CHIPS)
    ]


def flip(value, mask):
    return lax.ppermute(value, "dp", [(s, s ^ mask) for s in range(8)])


def from_plane(value, ahead):
    count = 2 * CHIPS
    return lax.ppermute(value, Z, [((d + 2 * ahead) % count, d) for d in range(count)])


def split_kernel(index_ref, grad_ref, out_ref):
    out_ref[0] = grad_ref[...]


def take_chunks(index, grad):
    return pl.pallas_call(
        split_kernel,
        grid_spec=pltpu.PrefetchScalarGridSpec(
            num_scalar_prefetch=1,
            grid=(4,),
            in_specs=[pl.BlockSpec((UNITS, BLK), lambda j, index: (0, index[j]))],
            out_specs=pl.BlockSpec((1, UNITS, BLK), lambda j, index: (j, 0, 0)),
        ),
        out_shape=jax.ShapeDtypeStruct((4, UNITS, BLK), BF16),
        compiler_params=params(),
        name="take_chunks",
    )(index, grad)


def core_sum_kernel(
    index_ref, near_ref, far_ref, near_in_ref, far_in_ref, hidden_ref, keep_ref, send_ref, units_ref
):
    keep_ref[0] = (near_ref[...].astype(F32) + near_in_ref[0].astype(F32)).astype(BF16)
    send_ref[0] = (far_ref[...].astype(F32) + far_in_ref[0].astype(F32)).astype(BF16)

    @pl.when(pl.program_id(0) == 0)
    def _():
        total = hidden_ref[0].astype(F32)
        for step in range(1, STEPS):
            total = total + hidden_ref[step].astype(F32)
        total = total.astype(BF16)
        for run in range(4):
            units_ref[run] = total


def core_sum(index, grad, received, hidden):
    whole = lambda shift: pl.BlockSpec((UNITS, BLK), lambda j, index: (0, index[j + shift]))
    part = lambda shift: pl.BlockSpec((1, UNITS, BLK), lambda j, index: (j + shift, 0, 0))
    every = pl.BlockSpec(hidden.shape, lambda j, index: (0, 0, 0))
    shape = jax.ShapeDtypeStruct((2, UNITS, BLK), BF16)
    return pl.pallas_call(
        core_sum_kernel,
        grid_spec=pltpu.PrefetchScalarGridSpec(
            num_scalar_prefetch=1,
            grid=(2,),
            in_specs=[whole(0), whole(2), part(0), part(2), every],
            out_specs=[part(0), part(0), every],
        ),
        out_shape=[shape, shape, jax.ShapeDtypeStruct(hidden.shape, BF16)],
        compiler_params=params(),
        name="core_sum",
    )(index, grad, grad, received, received, hidden)


def pair_sum_kernel(keep_ref, received_ref, out_ref):
    out_ref[...] = (keep_ref[0].astype(F32) + received_ref[0].astype(F32)).astype(BF16)


def pair_sum(keep, received):
    spec = pl.BlockSpec((1, UNITS, BLK), lambda i: (1, 0, 0))
    return pl.pallas_call(
        pair_sum_kernel,
        grid=(1,),
        in_specs=[spec, spec],
        out_specs=pl.BlockSpec((UNITS, BLK), lambda i: (0, 0)),
        out_shape=jax.ShapeDtypeStruct((UNITS, BLK), BF16),
        compiler_params=params(),
        cost_estimate=pl.CostEstimate(flops=10**11, bytes_accessed=10**9, transcendentals=0),
        name="pair_sum",
    )(keep, received)


def update_kernel(
    keep_ref, second_in_ref, third_in_ref, master_ref, moment_ref, second_ref, codes_ref, packed_ref
):
    for block in range(UNITS // BLK):
        rows = slice(block * BLK, (block + 1) * BLK)
        grad = (
            keep_ref[0, rows].astype(F32)
            + second_in_ref[0, rows].astype(F32)
            + third_in_ref[rows].astype(F32)
        )
        master = master_ref[rows]
        moment_new = beta_first * moment_ref[rows] + (1.0 - beta_first) * grad
        second_new = beta_second * second_ref[rows] + (1.0 - beta_second) * grad * grad
        moment_hat = moment_new / (1.0 - beta_first**adam_count)
        second_hat = second_new / (1.0 - beta_second**adam_count)
        weight = master - learn_rate * (
            moment_hat / (jnp.sqrt(second_hat) + adam_eps) + weight_decay * master
        )
        peak = jnp.max(jnp.max(jnp.abs(weight), axis=0, keepdims=True), axis=1, keepdims=True)
        scale = (peak + scale_eps).astype(BF16)
        codes = (weight / scale.astype(F32)).astype(BF16)
        codes_ref[rows] = codes
        packed_ref[rows] = codes
        packed_ref[UNITS + 16 * block : UNITS + 16 * (block + 1)] = jnp.broadcast_to(
            scale, (16, BLK)
        )


PACKED = UNITS + 16 * (UNITS // BLK)


def update(keep, second_in, third_in, master, moment, second):
    first = pl.BlockSpec((1, UNITS, BLK), lambda i: (0, 0, 0))
    flat = pl.BlockSpec((UNITS, BLK), lambda i: (0, 0))
    return pl.pallas_call(
        update_kernel,
        grid=(1,),
        in_specs=[first, first, flat, flat, flat, flat],
        out_specs=[flat, pl.BlockSpec((PACKED, BLK), lambda i: (0, 0))],
        out_shape=[
            jax.ShapeDtypeStruct((UNITS, BLK), BF16),
            jax.ShapeDtypeStruct((PACKED, BLK), BF16),
        ],
        compiler_params=params(),
        cost_estimate=pl.CostEstimate(flops=10**11, bytes_accessed=10**9, transcendentals=0),
        name="update",
    )(keep, second_in, third_in, master, moment, second)


def project_kernel(order_ref, same_ref, up_ref, two_low_ref, two_high_ref, down_ref, own_ref, other_ref, out_ref, sums):
    core = order_ref[CHIPS]
    start = 0
    for rows_ref in (same_ref, up_ref, two_low_ref, two_high_ref, down_ref):
        count = rows_ref.shape[0]
        for which, codes_ref in enumerate((own_ref, other_ref)):
            total = jnp.zeros((count * ROWS, BLK), F32)
            for block in range(UNITS // BLK):
                rows = rows_ref[:, :, block * BLK : (block + 1) * BLK].reshape(count * ROWS, BLK)
                codes = codes_ref[block * BLK : (block + 1) * BLK]
                scale = codes_ref[UNITS + 16 * block : UNITS + 16 * (block + 1)][:1].astype(F32)
                total = total + jnp.dot(rows, codes, preferred_element_type=F32) * scale
            sums[which, start : start + count] = total.astype(BF16).reshape(count, ROWS, BLK)
        start += count
    for place in range(CHIPS):
        row_block = order_ref[place]
        out_ref[place, core] = sums[0, row_block]
        out_ref[place, 1 - core] = sums[1, row_block]


def project(order, row_sets, own, other):
    rows = lambda x: pl.BlockSpec(x.shape, lambda i, order: (0, 0, 0))
    packed = pl.BlockSpec((PACKED, BLK), lambda i, order: (0, 0))
    return pl.pallas_call(
        project_kernel,
        grid_spec=pltpu.PrefetchScalarGridSpec(
            num_scalar_prefetch=1,
            grid=(1,),
            in_specs=[rows(x) for x in row_sets] + [packed, packed],
            out_specs=pl.BlockSpec((CHIPS, 2, ROWS, BLK), lambda i, order: (0, 0, 0, 0)),
            scratch_shapes=[pltpu.VMEM((2, CHIPS, ROWS, BLK), BF16)],
        ),
        out_shape=jax.ShapeDtypeStruct((CHIPS, 2, ROWS, BLK), BF16),
        compiler_params=params(),
        name="project",
    )(order, *row_sets, own, other)


def unit_sum_kernel(parts_ref, out_ref):
    total = parts_ref[0].astype(F32)
    for index in range(1, CHIPS):
        total = total + parts_ref[index].astype(F32)
    out_ref[...] = total.astype(BF16)


def unit_sum(parts):
    return pl.pallas_call(
        unit_sum_kernel,
        out_shape=jax.ShapeDtypeStruct((2, ROWS, BLK), BF16),
        compiler_params=params(),
        name="unit_sum",
    )(parts)


def finish_kernel(state_ref, attention_ref, mixed_ref, out_ref):
    for half in range(2):
        cols = slice(half * BLK, (half + 1) * BLK)
        out_ref[:, cols] = (
            state_ref[:, cols].astype(F32) + attention_ref[:, cols] + mixed_ref[half].astype(F32)
        ).astype(BF16)


def finish(state, attention, mixed):
    return pl.pallas_call(
        finish_kernel,
        out_shape=jax.ShapeDtypeStruct(state.shape, BF16),
        compiler_params=params(),
        name="finish",
    )(state, attention, mixed)


KEYS = ROWS * SLOTS
FRESH = 2 * STEPS * ROWS
SCALES_AT = 2 * KEYS + FRESH
CACHE_ROWS = SCALES_AT + 16


def pack_kernel(place_ref, keys_ref, values_ref, scale_ref, fresh_ref, out_ref):
    out_ref[:KEYS] = keys_ref[...]
    out_ref[KEYS : 2 * KEYS] = values_ref[...]
    width = fresh_ref.shape[1]
    wide = jnp.concatenate([fresh_ref[...].astype(F32)] * (HD // width), axis=1)
    lane = lax.broadcasted_iota(jnp.int32, wide.shape, 1)
    out_ref[2 * KEYS : SCALES_AT] = jnp.where(lane // width == place_ref[0], wide, 0.0).astype(BF16)
    spread = lax.broadcasted_iota(jnp.int32, (ROWS, KEYS), 1) // SLOTS
    spread = (spread == lax.broadcasted_iota(jnp.int32, (ROWS, KEYS), 0)).astype(BF16)
    lines = jnp.dot(scale_ref[...], spread, preferred_element_type=F32)
    slot = lax.broadcasted_iota(jnp.int32, lines.shape, 0) & (SLOTS - 1)
    lane = lax.broadcasted_iota(jnp.int32, lines.shape, 1) & (SLOTS - 1)
    lines = jnp.where(slot == lane, lines, 0.0)
    rows = [
        jnp.sum(lines[k * SLOTS : (k + 1) * SLOTS, i * HD : (i + 1) * HD], axis=0, keepdims=True)
        for k in range(2)
        for i in range(KEYS // HD)
    ]
    out_ref[SCALES_AT:] = jnp.concatenate(
        rows + [jnp.zeros((16 - len(rows), HD), F32)], axis=0
    ).astype(BF16)


def pack_caches(cache_k, cache_v, cache_scale, fresh_kv, place):
    vmem = pl.BlockSpec(memory_space=pltpu.VMEM)
    return pl.pallas_call(
        pack_kernel,
        in_specs=[pl.BlockSpec(memory_space=pltpu.SMEM)] + [vmem] * 4,
        out_specs=vmem,
        out_shape=jax.ShapeDtypeStruct((CACHE_ROWS, HD), BF16),
        compiler_params=params(),
        name="pack_caches",
    )(
        place[None],
        cache_k.reshape(KEYS, HD),
        cache_v.reshape(KEYS, HD),
        cache_scale.transpose(1, 2, 0).reshape(2 * SLOTS, ROWS),
        fresh_kv.reshape(FRESH, fresh_kv.shape[3]),
    )


def attend_kernel(lengths_ref, queries_ref, packed_ref, out_ref):
    inv = 1.0 / math.sqrt(HD)
    slots = QUADS * KEYS
    keys = packed_ref[:, :KEYS].reshape(slots, HD)
    values = packed_ref[:, KEYS : 2 * KEYS].reshape(slots, HD)
    fresh = packed_ref[0, 2 * KEYS : SCALES_AT].astype(F32)
    for place in range(1, QUADS):
        fresh = fresh + packed_ref[place, 2 * KEYS : SCALES_AT].astype(F32)
    new_keys = fresh.astype(BF16)
    new_values = pltpu.roll(fresh, FRESH - 1, 0).astype(BF16)
    scales = packed_ref[:, SCALES_AT:].astype(F32)
    lines = KEYS // HD
    key_scale = jnp.concatenate(
        [scales[p, i : i + 1] for p in range(QUADS) for i in range(lines)], axis=1
    )
    value_scale = jnp.concatenate(
        [scales[p, lines + i : lines + i + 1] for p in range(QUADS) for i in range(lines)], axis=1
    )
    row = lax.broadcasted_iota(jnp.int32, (ROWS, ROWS), 0)
    column = lax.broadcasted_iota(jnp.int32, (ROWS, ROWS), 1)
    length = jnp.where(row == column, lengths_ref[...].astype(F32), 0.0)
    length = jnp.sum(length, axis=1, keepdims=True).astype(jnp.int32)
    lane = lax.broadcasted_iota(jnp.int32, (ROWS, slots), 1)
    row = lax.broadcasted_iota(jnp.int32, (ROWS, slots), 0)
    slot = (lane // KEYS) * SLOTS + (lane & (SLOTS - 1))
    live = ((lane // SLOTS) & (ROWS - 1)) == row
    live = live & (slot < length)
    ahead = slot - length
    window = CACHE - SINK
    lane = lax.broadcasted_iota(jnp.int32, (ROWS, FRESH), 1)
    row = lax.broadcasted_iota(jnp.int32, (ROWS, FRESH), 0)
    mine = (((lane // 2) & (ROWS - 1)) == row) & ((lane & 1) == 0)
    old_sum = [jnp.zeros((ROWS, slots), F32) for _ in range(2)]
    new_sum = [jnp.zeros((ROWS, FRESH), F32) for _ in range(2)]
    for step in range(STEPS):
        evicted = ahead == step
        for turn in range(1, (4 * CACHE + STEPS) // window + 1):
            evicted = evicted | (ahead == step - turn * window)
        live = live & jnp.logical_not(evicted & (slot >= SINK))
        seen = mine & (lane // (2 * ROWS) <= step)
        for head in range(2):
            query = queries_ref[step, :, head * HD : (head + 1) * HD]
            across = (((1,), (1,)), ((), ()))
            old = lax.dot_general(query, keys, across, preferred_element_type=F32)
            old = jnp.where(live, old * (key_scale * inv), -jnp.inf)
            new = lax.dot_general(query, new_keys, across, preferred_element_type=F32) * inv
            new = jnp.where(seen, new, -jnp.inf)
            top = jnp.maximum(
                jnp.max(old, axis=1, keepdims=True), jnp.max(new, axis=1, keepdims=True)
            )
            old = jnp.exp(old - top)
            new = jnp.exp(new - top)
            share = 1.0 / (jnp.sum(old, axis=1, keepdims=True) + jnp.sum(new, axis=1, keepdims=True))
            old_sum[head] = old_sum[head] + old * share
            new_sum[head] = new_sum[head] + new * share
    for head in range(2):
        old = (old_sum[head] * value_scale).astype(BF16)
        new = new_sum[head].astype(BF16)
        out_ref[:, head * HD : (head + 1) * HD] = jnp.dot(
            old, values, preferred_element_type=F32
        ) + jnp.dot(new, new_values, preferred_element_type=F32)


def attend(lengths, queries, packed):
    return pl.pallas_call(
        attend_kernel,
        out_shape=jax.ShapeDtypeStruct((ROWS, 2 * HD), F32),
        compiler_params=params(),
        name="attend",
    )(lengths[None], queries, packed)


def shards(
    grad_partials,
    master,
    moment,
    second,
    state,
    hidden,
    queries,
    fresh_kv,
    cache_k,
    cache_v,
    cache_scale,
    lengths,
):
    dp = lax.axis_index("dp")
    tp = lax.axis_index("tp")
    core, low = dp % 2, dp // 2
    plane = lax.axis_index("grp") * 4 + low
    grad = grad_partials[0]

    owners = low ^ jnp.array([0, 2, 1, 3], jnp.int32)
    outgoing = take_chunks(2 * owners + 1 - core, grad)
    received = flip(outgoing, 1)
    keep, send, units = core_sum(2 * owners + core, grad, received, hidden)
    second_in = flip(send, 2)

    same = lax.all_to_all(units, "grp", 0, 0)

    caches = pack_caches(cache_k, cache_v, cache_scale, fresh_kv, tp % QUADS)
    caches = jnp.broadcast_to(caches, (QUADS,) + caches.shape)
    caches, _ = lax.optimization_barrier((caches, send))
    quads = [[QUADS * x + y for y in range(QUADS)] for x in range(QUADS)]
    packed = lax.all_to_all(caches, "tp", 0, 0, axis_index_groups=quads)

    third = pair_sum(keep, second_in)
    third_in = flip(third, 4)
    same, _ = lax.optimization_barrier((same, third))
    up = from_plane(same, 1)
    down = from_plane(same, -1)
    two_low = from_plane(same[:2], 2)
    two_high = from_plane(same[2:], -2)
    attention = attend(lengths, queries, packed)

    codes, own = update(keep, second_in, third_in, master, moment, second)
    own, up, down, two_low, two_high = lax.optimization_barrier(
        (own, up, down, two_low, two_high)
    )
    other = flip(own, 1)

    row_at = lax.dynamic_index_in_dim(jnp.array(ROW_AT), plane, 0, keepdims=False)
    order = ((row_at - low) & 3) * 4 + row_at // 4
    order = jnp.concatenate([order, core[None]]).astype(jnp.int32)
    parts = project(order, (same, up, two_low, two_high, down), own, other)
    parts = lax.all_to_all(parts, "tp", 0, 0)
    mixed = lax.ppermute(unit_sum(parts), ALL, home_pairs())
    return (codes, finish(state, attention, mixed))


def solution(mesh):
    return jax.shard_map(
        shards,
        mesh=mesh,
        in_specs=(
            P("dp", "tp", "grp"),
            P("tp", ("grp", "dp")),
            P("tp", ("grp", "dp")),
            P("tp", ("grp", "dp")),
            P(("grp", "dp"), "tp"),
            P(None, ("grp", "dp"), "tp"),
            P(None, ("grp", "dp"), "tp"),
            P(None, ("grp", "dp"), None, "tp"),
            P(("grp", "dp"), "tp", None),
            P(("grp", "dp"), "tp", None),
            P(("grp", "dp"), None, "tp"),
            P(("grp", "dp")),
        ),
        out_specs=(P("tp", ("grp", "dp")), P(("grp", "dp"), "tp")),
        check_vma=False,
    )
```

```python
import math

import jax
import jax.numpy as jnp
import numpy as np
from jax import lax
from jax.experimental import pallas as pl
from jax.experimental.pallas import tpu as pltpu
from jax.sharding import PartitionSpec as P

HD = 128
BLK = 128
CACHE = 32
SINK = 4
STEPS = 4
QUADS = 4
CHIPS = 16
ROWS = 32
UNITS = 1024
SLOTS = CACHE // QUADS

beta_first = 0.9
beta_second = 0.95
adam_eps = 1e-08
weight_decay = 0.1
learn_rate = 0.01
adam_count = 100.0
scale_eps = 1e-06

Z = ("grp", "dp")
ALL = ("grp", "dp", "tp")
F32 = jnp.float32
BF16 = jnp.bfloat16
VMEM_LIMIT = 48 * 1024 * 1024


def params():
    return pltpu.CompilerParams(vmem_limit_bytes=VMEM_LIMIT)


def ring_distance(a, b, n):
    d = abs(a - b) % n
    return min(d, n - d)


def row_places():
    places = []
    for c in range(CHIPS):
        by_z = sorted(range(CHIPS), key=lambda r: (-ring_distance(c, r, CHIPS), r))
        by_xy = sorted(
            range(CHIPS),
            key=lambda p: (ring_distance(p // 4, c // 4, 4) + ring_distance(p % 4, c % 4, 4), p),
        )
        place = [0] * CHIPS
        for r, p in zip(by_z, by_xy):
            place[r] = p
        places.append(place)
    return places


PLACES = row_places()
ROW_AT = np.argsort(np.array(PLACES), axis=1).astype(np.int32)


def home_pairs():
    return [
        ((c * 2 + b) * CHIPS + PLACES[c][r], (r * 2 + b) * CHIPS + c)
        for c in range(CHIPS)
        for b in range(2)
        for r in range(CHIPS)
    ]


def flip(value, mask):
    return lax.ppermute(value, "dp", [(s, s ^ mask) for s in range(8)])


def from_plane(value, ahead):
    pairs = [
        ((plane + ahead(plane)) % CHIPS * 2 + core, plane * 2 + core)
        for plane in range(CHIPS)
        for core in range(2)
    ]
    return lax.ppermute(value, Z, pairs)


def swap(value, mask):
    return lax.ppermute(value, "tp", [(s, s ^ mask) for s in range(CHIPS)])


def split_kernel(index_ref, grad_ref, out_ref):
    out_ref[0] = grad_ref[...]


def take_chunks(index, grad):
    return pl.pallas_call(
        split_kernel,
        grid_spec=pltpu.PrefetchScalarGridSpec(
            num_scalar_prefetch=1,
            grid=(4,),
            in_specs=[pl.BlockSpec((UNITS, BLK), lambda j, index: (0, index[j]))],
            out_specs=pl.BlockSpec((1, UNITS, BLK), lambda j, index: (j, 0, 0)),
        ),
        out_shape=jax.ShapeDtypeStruct((4, UNITS, BLK), BF16),
        compiler_params=params(),
        name="take_chunks",
    )(index, grad)


def core_sum_kernel(
    index_ref, near_ref, far_ref, near_in_ref, far_in_ref, hidden_ref, keep_ref, send_ref, units_ref
):
    keep_ref[0] = (near_ref[...].astype(F32) + near_in_ref[0].astype(F32)).astype(BF16)
    send_ref[0] = (far_ref[...].astype(F32) + far_in_ref[0].astype(F32)).astype(BF16)

    @pl.when(pl.program_id(0) == 0)
    def _():
        total = hidden_ref[0].astype(F32)
        for step in range(1, STEPS):
            total = total + hidden_ref[step].astype(F32)
        total = total.astype(BF16)
        for run in range(4):
            units_ref[run] = total


def core_sum(index, grad, received, hidden):
    whole = lambda shift: pl.BlockSpec((UNITS, BLK), lambda j, index: (0, index[j + shift]))
    part = lambda shift: pl.BlockSpec((1, UNITS, BLK), lambda j, index: (j + shift, 0, 0))
    every = pl.BlockSpec(hidden.shape, lambda j, index: (0, 0, 0))
    shape = jax.ShapeDtypeStruct((2, UNITS, BLK), BF16)
    return pl.pallas_call(
        core_sum_kernel,
        grid_spec=pltpu.PrefetchScalarGridSpec(
            num_scalar_prefetch=1,
            grid=(2,),
            in_specs=[whole(0), whole(2), part(0), part(2), every],
            out_specs=[part(0), part(0), every],
        ),
        out_shape=[shape, shape, jax.ShapeDtypeStruct(hidden.shape, BF16)],
        compiler_params=params(),
        name="core_sum",
    )(index, grad, grad, received, received, hidden)


def pair_sum_kernel(keep_ref, received_ref, out_ref):
    out_ref[...] = (keep_ref[0].astype(F32) + received_ref[0].astype(F32)).astype(BF16)


def pair_sum(keep, received):
    spec = pl.BlockSpec((1, UNITS, BLK), lambda i: (1, 0, 0))
    return pl.pallas_call(
        pair_sum_kernel,
        grid=(1,),
        in_specs=[spec, spec],
        out_specs=pl.BlockSpec((UNITS, BLK), lambda i: (0, 0)),
        out_shape=jax.ShapeDtypeStruct((UNITS, BLK), BF16),
        compiler_params=params(),
        cost_estimate=pl.CostEstimate(flops=10**11, bytes_accessed=10**9, transcendentals=0),
        name="pair_sum",
    )(keep, received)


def update_kernel(
    keep_ref, second_in_ref, third_in_ref, master_ref, moment_ref, second_ref, codes_ref, packed_ref
):
    for block in range(UNITS // BLK):
        rows = slice(block * BLK, (block + 1) * BLK)
        grad = (
            keep_ref[0, rows].astype(F32)
            + second_in_ref[0, rows].astype(F32)
            + third_in_ref[rows].astype(F32)
        )
        master = master_ref[rows]
        moment_new = beta_first * moment_ref[rows] + (1.0 - beta_first) * grad
        second_new = beta_second * second_ref[rows] + (1.0 - beta_second) * grad * grad
        moment_hat = moment_new / (1.0 - beta_first**adam_count)
        second_hat = second_new / (1.0 - beta_second**adam_count)
        weight = master - learn_rate * (
            moment_hat / (jnp.sqrt(second_hat) + adam_eps) + weight_decay * master
        )
        peak = jnp.max(jnp.max(jnp.abs(weight), axis=0, keepdims=True), axis=1, keepdims=True)
        scale = (peak + scale_eps).astype(BF16)
        codes = (weight / scale.astype(F32)).astype(BF16)
        codes_ref[rows] = codes
        packed_ref[rows] = codes
        packed_ref[UNITS + 16 * block : UNITS + 16 * (block + 1)] = jnp.broadcast_to(
            scale, (16, BLK)
        )


PACKED = UNITS + 16 * (UNITS // BLK)


def update(keep, second_in, third_in, master, moment, second):
    first = pl.BlockSpec((1, UNITS, BLK), lambda i: (0, 0, 0))
    flat = pl.BlockSpec((UNITS, BLK), lambda i: (0, 0))
    return pl.pallas_call(
        update_kernel,
        grid=(1,),
        in_specs=[first, first, flat, flat, flat, flat],
        out_specs=[flat, pl.BlockSpec((PACKED, BLK), lambda i: (0, 0))],
        out_shape=[
            jax.ShapeDtypeStruct((UNITS, BLK), BF16),
            jax.ShapeDtypeStruct((PACKED, BLK), BF16),
        ],
        compiler_params=params(),
        cost_estimate=pl.CostEstimate(flops=10**11, bytes_accessed=10**9, transcendentals=0),
        name="update",
    )(keep, second_in, third_in, master, moment, second)


def project_kernel(
    order_ref, same_ref, up_ref, two_ref, down_ref, own_ref, other_ref, out_ref, sums
):
    core = order_ref[CHIPS]
    start = 0
    for rows_ref in (same_ref, up_ref, two_ref, down_ref):
        count = rows_ref.shape[0]
        for which, codes_ref in enumerate((own_ref, other_ref)):
            total = jnp.zeros((count * ROWS, BLK), F32)
            for block in range(UNITS // BLK):
                rows = rows_ref[:, :, block * BLK : (block + 1) * BLK].reshape(count * ROWS, BLK)
                codes = codes_ref[block * BLK : (block + 1) * BLK]
                scale = codes_ref[UNITS + 16 * block : UNITS + 16 * (block + 1)][:1].astype(F32)
                total = total + jnp.dot(rows, codes, preferred_element_type=F32) * scale
            sums[which, start : start + count] = total.astype(BF16).reshape(count, ROWS, BLK)
        start += count
    for place in range(CHIPS):
        row_block = order_ref[place]
        out_ref[place, core] = sums[0, row_block]
        out_ref[place, 1 - core] = sums[1, row_block]


def project(order, row_sets, own, other):
    rows = lambda x: pl.BlockSpec(x.shape, lambda i, order: (0, 0, 0))
    packed = pl.BlockSpec((PACKED, BLK), lambda i, order: (0, 0))
    return pl.pallas_call(
        project_kernel,
        grid_spec=pltpu.PrefetchScalarGridSpec(
            num_scalar_prefetch=1,
            grid=(1,),
            in_specs=[rows(x) for x in row_sets] + [packed, packed],
            out_specs=pl.BlockSpec((CHIPS, 2, ROWS, BLK), lambda i, order: (0, 0, 0, 0)),
            scratch_shapes=[pltpu.VMEM((2, CHIPS, ROWS, BLK), BF16)],
        ),
        out_shape=jax.ShapeDtypeStruct((CHIPS, 2, ROWS, BLK), BF16),
        compiler_params=params(),
        name="project",
    )(order, *row_sets, own, other)


def unit_sum_kernel(parts_ref, out_ref):
    total = parts_ref[0].astype(F32)
    for index in range(1, CHIPS):
        total = total + parts_ref[index].astype(F32)
    out_ref[...] = total.astype(BF16)


def unit_sum(parts):
    return pl.pallas_call(
        unit_sum_kernel,
        out_shape=jax.ShapeDtypeStruct((2, ROWS, BLK), BF16),
        compiler_params=params(),
        name="unit_sum",
    )(parts)


def finish_kernel(state_ref, attention_ref, mixed_ref, out_ref):
    for half in range(2):
        cols = slice(half * BLK, (half + 1) * BLK)
        out_ref[:, cols] = (
            state_ref[:, cols].astype(F32) + attention_ref[:, cols] + mixed_ref[half].astype(F32)
        ).astype(BF16)


def finish(state, attention, mixed):
    return pl.pallas_call(
        finish_kernel,
        out_shape=jax.ShapeDtypeStruct(state.shape, BF16),
        compiler_params=params(),
        name="finish",
    )(state, attention, mixed)


KEYS = ROWS * SLOTS
FRESH = 2 * STEPS * ROWS
SCALES_AT = 2 * KEYS + FRESH
CACHE_ROWS = SCALES_AT + 16


def pack_kernel(place_ref, keys_ref, values_ref, scale_ref, fresh_ref, out_ref):
    out_ref[:KEYS] = keys_ref[...]
    out_ref[KEYS : 2 * KEYS] = values_ref[...]
    width = fresh_ref.shape[1]
    wide = jnp.concatenate([fresh_ref[...].astype(F32)] * (HD // width), axis=1)
    lane = lax.broadcasted_iota(jnp.int32, wide.shape, 1)
    out_ref[2 * KEYS : SCALES_AT] = jnp.where(lane // width == place_ref[0], wide, 0.0).astype(BF16)
    spread = lax.broadcasted_iota(jnp.int32, (ROWS, KEYS), 1) // SLOTS
    spread = (spread == lax.broadcasted_iota(jnp.int32, (ROWS, KEYS), 0)).astype(BF16)
    lines = jnp.dot(scale_ref[...], spread, preferred_element_type=F32)
    slot = lax.broadcasted_iota(jnp.int32, lines.shape, 0) & (SLOTS - 1)
    lane = lax.broadcasted_iota(jnp.int32, lines.shape, 1) & (SLOTS - 1)
    lines = jnp.where(slot == lane, lines, 0.0)
    rows = [
        jnp.sum(lines[k * SLOTS : (k + 1) * SLOTS, i * HD : (i + 1) * HD], axis=0, keepdims=True)
        for k in range(2)
        for i in range(KEYS // HD)
    ]
    out_ref[SCALES_AT:] = jnp.concatenate(
        rows + [jnp.zeros((16 - len(rows), HD), F32)], axis=0
    ).astype(BF16)


def pack_caches(cache_k, cache_v, cache_scale, fresh_kv, place):
    vmem = pl.BlockSpec(memory_space=pltpu.VMEM)
    return pl.pallas_call(
        pack_kernel,
        in_specs=[pl.BlockSpec(memory_space=pltpu.SMEM)] + [vmem] * 4,
        out_specs=vmem,
        out_shape=jax.ShapeDtypeStruct((CACHE_ROWS, HD), BF16),
        compiler_params=params(),
        name="pack_caches",
    )(
        place[None],
        cache_k.reshape(KEYS, HD),
        cache_v.reshape(KEYS, HD),
        cache_scale.transpose(1, 2, 0).reshape(2 * SLOTS, ROWS),
        fresh_kv.reshape(FRESH, fresh_kv.shape[3]),
    )


def attend_kernel(place_ref, lengths_ref, queries_ref, *refs):
    packed_refs, out_ref = refs[:QUADS], refs[QUADS]
    inv = 1.0 / math.sqrt(HD)
    slots = QUADS * KEYS
    keys = jnp.concatenate([ref[:KEYS] for ref in packed_refs], axis=0)
    values = jnp.concatenate([ref[KEYS : 2 * KEYS] for ref in packed_refs], axis=0)
    fresh = packed_refs[0][2 * KEYS : SCALES_AT].astype(F32)
    for ref in packed_refs[1:]:
        fresh = fresh + ref[2 * KEYS : SCALES_AT].astype(F32)
    new_keys = fresh.astype(BF16)
    new_values = pltpu.roll(fresh, FRESH - 1, 0).astype(BF16)
    scales = [ref[SCALES_AT:].astype(F32) for ref in packed_refs]
    lines = KEYS // HD
    key_scale = jnp.concatenate(
        [scales[p][i : i + 1] for p in range(QUADS) for i in range(lines)], axis=1
    )
    value_scale = jnp.concatenate(
        [scales[p][lines + i : lines + i + 1] for p in range(QUADS) for i in range(lines)], axis=1
    )
    row = lax.broadcasted_iota(jnp.int32, (ROWS, ROWS), 0)
    column = lax.broadcasted_iota(jnp.int32, (ROWS, ROWS), 1)
    length = jnp.where(row == column, lengths_ref[...].astype(F32), 0.0)
    length = jnp.sum(length, axis=1, keepdims=True).astype(jnp.int32)
    lane = lax.broadcasted_iota(jnp.int32, (ROWS, slots), 1)
    row = lax.broadcasted_iota(jnp.int32, (ROWS, slots), 0)
    slot = ((lane // KEYS) ^ place_ref[0]) * SLOTS + (lane & (SLOTS - 1))
    live = ((lane // SLOTS) & (ROWS - 1)) == row
    live = live & (slot < length)
    ahead = slot - length
    window = CACHE - SINK
    lane = lax.broadcasted_iota(jnp.int32, (ROWS, FRESH), 1)
    row = lax.broadcasted_iota(jnp.int32, (ROWS, FRESH), 0)
    mine = (((lane // 2) & (ROWS - 1)) == row) & ((lane & 1) == 0)
    old_sum = [jnp.zeros((ROWS, slots), F32) for _ in range(2)]
    new_sum = [jnp.zeros((ROWS, FRESH), F32) for _ in range(2)]
    for step in range(STEPS):
        evicted = ahead == step
        for turn in range(1, (4 * CACHE + STEPS) // window + 1):
            evicted = evicted | (ahead == step - turn * window)
        live = live & jnp.logical_not(evicted & (slot >= SINK))
        seen = mine & (lane // (2 * ROWS) <= step)
        for head in range(2):
            query = queries_ref[step, :, head * HD : (head + 1) * HD]
            across = (((1,), (1,)), ((), ()))
            old = lax.dot_general(query, keys, across, preferred_element_type=F32)
            old = jnp.where(live, old * (key_scale * inv), -jnp.inf)
            new = lax.dot_general(query, new_keys, across, preferred_element_type=F32) * inv
            new = jnp.where(seen, new, -jnp.inf)
            top = jnp.maximum(
                jnp.max(old, axis=1, keepdims=True), jnp.max(new, axis=1, keepdims=True)
            )
            old = jnp.exp(old - top)
            new = jnp.exp(new - top)
            share = 1.0 / (jnp.sum(old, axis=1, keepdims=True) + jnp.sum(new, axis=1, keepdims=True))
            old_sum[head] = old_sum[head] + old * share
            new_sum[head] = new_sum[head] + new * share
    for head in range(2):
        old = (old_sum[head] * value_scale).astype(BF16)
        new = new_sum[head].astype(BF16)
        out_ref[:, head * HD : (head + 1) * HD] = jnp.dot(
            old, values, preferred_element_type=F32
        ) + jnp.dot(new, new_values, preferred_element_type=F32)


def attend(place, lengths, queries, packed):
    vmem = pl.BlockSpec(memory_space=pltpu.VMEM)
    return pl.pallas_call(
        attend_kernel,
        in_specs=[pl.BlockSpec(memory_space=pltpu.SMEM)] + [vmem] * (2 + QUADS),
        out_specs=vmem,
        out_shape=jax.ShapeDtypeStruct((ROWS, 2 * HD), F32),
        compiler_params=params(),
        name="attend",
    )(place[None], lengths[None], queries, *packed)


def shards(
    grad_partials,
    master,
    moment,
    second,
    state,
    hidden,
    queries,
    fresh_kv,
    cache_k,
    cache_v,
    cache_scale,
    lengths,
):
    dp = lax.axis_index("dp")
    tp = lax.axis_index("tp")
    core, low = dp % 2, dp // 2
    plane = lax.axis_index("grp") * 4 + low
    grad = grad_partials[0]

    owners = low ^ jnp.array([0, 2, 1, 3], jnp.int32)
    outgoing = take_chunks(2 * owners + 1 - core, grad)
    received = flip(outgoing, 1)
    keep, send, units = core_sum(2 * owners + core, grad, received, hidden)
    second_in = flip(send, 2)

    same = lax.all_to_all(units, "grp", 0, 0)

    third = pair_sum(keep, second_in)
    third_in = flip(third, 4)
    same, _ = lax.optimization_barrier((same, third))
    place = tp % QUADS
    caches = pack_caches(cache_k, cache_v, cache_scale, fresh_kv, place)
    caches, _, _ = lax.optimization_barrier((caches, third, same))
    first = swap(caches, 1)
    two = from_plane(same, lambda plane: 2 if plane % 2 == 0 else -2)
    up = from_plane(same, lambda plane: 1)
    down = from_plane(same, lambda plane: -1)

    codes, own = update(keep, second_in, third_in, master, moment, second)
    own, two, up, down, first = lax.optimization_barrier((own, two, up, down, first))
    other = flip(own, 1)

    row_at = lax.dynamic_index_in_dim(jnp.array(ROW_AT), plane, 0, keepdims=False)
    order = ((row_at - low) & 3) * 4 + row_at // 4
    order = jnp.concatenate([order, core[None]]).astype(jnp.int32)
    parts = project(order, (same, up, two, down), own, other)
    caches, parts = lax.optimization_barrier((caches, parts))
    packed = [caches, first] + [swap(caches, mask) for mask in range(2, QUADS)]
    attention = attend(place, lengths, queries, packed)
    parts = lax.all_to_all(parts, "tp", 0, 0)
    mixed = lax.ppermute(unit_sum(parts), ALL, home_pairs())
    return (codes, finish(state, attention, mixed))


def solution(mesh):
    return jax.shard_map(
        shards,
        mesh=mesh,
        in_specs=(
            P("dp", "tp", "grp"),
            P("tp", ("grp", "dp")),
            P("tp", ("grp", "dp")),
            P("tp", ("grp", "dp")),
            P(("grp", "dp"), "tp"),
            P(None, ("grp", "dp"), "tp"),
            P(None, ("grp", "dp"), "tp"),
            P(None, ("grp", "dp"), None, "tp"),
            P(("grp", "dp"), "tp", None),
            P(("grp", "dp"), "tp", None),
            P(("grp", "dp"), None, "tp"),
            P(("grp", "dp")),
        ),
        out_specs=(P("tp", ("grp", "dp")), P(("grp", "dp"), "tp")),
        check_vma=False,
    )
```

```python
import math

import jax
import jax.numpy as jnp
import numpy as np
from jax import lax
from jax.experimental import pallas as pl
from jax.experimental.pallas import tpu as pltpu
from jax.sharding import PartitionSpec as P

HD = 128
BLK = 128
CACHE = 32
SINK = 4
STEPS = 4
QUADS = 4
CHIPS = 16
ROWS = 32
UNITS = 1024
SLOTS = CACHE // QUADS

beta_first = 0.9
beta_second = 0.95
adam_eps = 1e-08
weight_decay = 0.1
learn_rate = 0.01
adam_count = 100.0
scale_eps = 1e-06

Z = ("grp", "dp")
ALL = ("grp", "dp", "tp")
F32 = jnp.float32
BF16 = jnp.bfloat16
VMEM_LIMIT = 48 * 1024 * 1024


def params():
    return pltpu.CompilerParams(vmem_limit_bytes=VMEM_LIMIT)


def ring_distance(a, b, n):
    d = abs(a - b) % n
    return min(d, n - d)


def row_places():
    places = []
    for c in range(CHIPS):
        by_z = sorted(range(CHIPS), key=lambda r: (-ring_distance(c, r, CHIPS), r))
        by_xy = sorted(
            range(CHIPS),
            key=lambda p: (ring_distance(p // 4, c // 4, 4) + ring_distance(p % 4, c % 4, 4), p),
        )
        place = [0] * CHIPS
        for r, p in zip(by_z, by_xy):
            place[r] = p
        places.append(place)
    return places


PLACES = row_places()
ROW_AT = np.argsort(np.array(PLACES), axis=1).astype(np.int32)


def home_pairs():
    return [
        ((c * 2 + b) * CHIPS + PLACES[c][r], (r * 2 + b) * CHIPS + c)
        for c in range(CHIPS)
        for b in range(2)
        for r in range(CHIPS)
    ]


def flip(value, mask):
    return lax.ppermute(value, "dp", [(s, s ^ mask) for s in range(8)])


def from_plane(value, ahead):
    pairs = [
        ((plane + ahead(plane)) % CHIPS * 2 + core, plane * 2 + core)
        for plane in range(CHIPS)
        for core in range(2)
    ]
    return lax.ppermute(value, Z, pairs)


def swap(value, mask):
    return lax.ppermute(value, "tp", [(s, s ^ mask) for s in range(CHIPS)])


def chunk_at(j, dp, core):
    return 2 * ((dp >> 1) ^ (((j & 1) << 1) | (j >> 1))) + core


def split_kernel(dp_ref, grad_ref, out_ref):
    out_ref[0] = grad_ref[...]


def take_chunks(dp, grad):
    return pl.pallas_call(
        split_kernel,
        grid_spec=pltpu.PrefetchScalarGridSpec(
            num_scalar_prefetch=1,
            grid=(4,),
            in_specs=[
                pl.BlockSpec(
                    (UNITS, BLK), lambda j, dp: (0, chunk_at(j, dp[0], 1 - (dp[0] & 1)))
                )
            ],
            out_specs=pl.BlockSpec((1, UNITS, BLK), lambda j, dp: (j, 0, 0)),
        ),
        out_shape=jax.ShapeDtypeStruct((4, UNITS, BLK), BF16),
        compiler_params=params(),
        name="take_chunks",
    )(dp[None], grad)


def core_sum_kernel(
    dp_ref, near_ref, far_ref, near_in_ref, far_in_ref, hidden_ref, keep_ref, send_ref, units_ref
):
    keep_ref[0] = (near_ref[...].astype(F32) + near_in_ref[0].astype(F32)).astype(BF16)
    send_ref[0] = (far_ref[...].astype(F32) + far_in_ref[0].astype(F32)).astype(BF16)

    @pl.when(pl.program_id(0) == 0)
    def _():
        total = hidden_ref[0].astype(F32)
        for step in range(1, STEPS):
            total = total + hidden_ref[step].astype(F32)
        total = total.astype(BF16)
        for run in range(4):
            units_ref[run] = total


def core_sum(dp, grad, received, hidden):
    whole = lambda shift: pl.BlockSpec(
        (UNITS, BLK), lambda j, dp: (0, chunk_at(j + shift, dp[0], dp[0] & 1))
    )
    part = lambda shift: pl.BlockSpec((1, UNITS, BLK), lambda j, index: (j + shift, 0, 0))
    every = pl.BlockSpec(hidden.shape, lambda j, index: (0, 0, 0))
    shape = jax.ShapeDtypeStruct((2, UNITS, BLK), BF16)
    return pl.pallas_call(
        core_sum_kernel,
        grid_spec=pltpu.PrefetchScalarGridSpec(
            num_scalar_prefetch=1,
            grid=(2,),
            in_specs=[whole(0), whole(2), part(0), part(2), every],
            out_specs=[part(0), part(0), every],
        ),
        out_shape=[shape, shape, jax.ShapeDtypeStruct(hidden.shape, BF16)],
        compiler_params=params(),
        name="core_sum",
    )(dp[None], grad, grad, received, received, hidden)


def pair_sum_kernel(keep_ref, received_ref, out_ref):
    out_ref[...] = (keep_ref[0].astype(F32) + received_ref[0].astype(F32)).astype(BF16)


def pair_sum(keep, received):
    spec = pl.BlockSpec((1, UNITS, BLK), lambda i: (1, 0, 0))
    return pl.pallas_call(
        pair_sum_kernel,
        grid=(1,),
        in_specs=[spec, spec],
        out_specs=pl.BlockSpec((UNITS, BLK), lambda i: (0, 0)),
        out_shape=jax.ShapeDtypeStruct((UNITS, BLK), BF16),
        compiler_params=params(),
        cost_estimate=pl.CostEstimate(flops=10**11, bytes_accessed=10**9, transcendentals=0),
        name="pair_sum",
    )(keep, received)


def update_kernel(
    keep_ref, second_in_ref, third_in_ref, master_ref, moment_ref, second_ref, codes_ref, packed_ref
):
    for block in range(UNITS // BLK):
        rows = slice(block * BLK, (block + 1) * BLK)
        grad = (
            keep_ref[0, rows].astype(F32)
            + second_in_ref[0, rows].astype(F32)
            + third_in_ref[rows].astype(F32)
        )
        master = master_ref[rows]
        moment_new = beta_first * moment_ref[rows] + (1.0 - beta_first) * grad
        second_new = beta_second * second_ref[rows] + (1.0 - beta_second) * grad * grad
        moment_hat = moment_new / (1.0 - beta_first**adam_count)
        second_hat = second_new / (1.0 - beta_second**adam_count)
        weight = master - learn_rate * (
            moment_hat / (jnp.sqrt(second_hat) + adam_eps) + weight_decay * master
        )
        peak = jnp.max(jnp.max(jnp.abs(weight), axis=0, keepdims=True), axis=1, keepdims=True)
        scale = (peak + scale_eps).astype(BF16)
        codes = (weight / scale.astype(F32)).astype(BF16)
        codes_ref[rows] = codes
        packed_ref[rows] = codes
        packed_ref[UNITS + 16 * block : UNITS + 16 * (block + 1)] = jnp.broadcast_to(
            scale, (16, BLK)
        )


PACKED = UNITS + 16 * (UNITS // BLK)


def update(keep, second_in, third_in, master, moment, second):
    first = pl.BlockSpec((1, UNITS, BLK), lambda i: (0, 0, 0))
    flat = pl.BlockSpec((UNITS, BLK), lambda i: (0, 0))
    return pl.pallas_call(
        update_kernel,
        grid=(1,),
        in_specs=[first, first, flat, flat, flat, flat],
        out_specs=[flat, pl.BlockSpec((PACKED, BLK), lambda i: (0, 0))],
        out_shape=[
            jax.ShapeDtypeStruct((UNITS, BLK), BF16),
            jax.ShapeDtypeStruct((PACKED, BLK), BF16),
        ],
        compiler_params=params(),
        cost_estimate=pl.CostEstimate(flops=10**11, bytes_accessed=10**9, transcendentals=0),
        name="update",
    )(keep, second_in, third_in, master, moment, second)


def project_kernel(
    order_ref, same_ref, up_ref, two_ref, down_ref, own_ref, other_ref, out_ref, sums
):
    core = order_ref[CHIPS]
    start = 0
    for rows_ref in (same_ref, up_ref, two_ref, down_ref):
        count = rows_ref.shape[0]
        for which, codes_ref in enumerate((own_ref, other_ref)):
            total = jnp.zeros((count * ROWS, BLK), F32)
            for block in range(UNITS // BLK):
                rows = rows_ref[:, :, block * BLK : (block + 1) * BLK].reshape(count * ROWS, BLK)
                codes = codes_ref[block * BLK : (block + 1) * BLK]
                scale = codes_ref[UNITS + 16 * block : UNITS + 16 * (block + 1)][:1].astype(F32)
                total = total + jnp.dot(rows, codes, preferred_element_type=F32) * scale
            sums[which, start : start + count] = total.astype(BF16).reshape(count, ROWS, BLK)
        start += count
    for place in range(CHIPS):
        row_block = order_ref[place]
        out_ref[place, core] = sums[0, row_block]
        out_ref[place, 1 - core] = sums[1, row_block]


def project(order, row_sets, own, other):
    rows = lambda x: pl.BlockSpec(x.shape, lambda i, order: (0, 0, 0))
    packed = pl.BlockSpec((PACKED, BLK), lambda i, order: (0, 0))
    return pl.pallas_call(
        project_kernel,
        grid_spec=pltpu.PrefetchScalarGridSpec(
            num_scalar_prefetch=1,
            grid=(1,),
            in_specs=[rows(x) for x in row_sets] + [packed, packed],
            out_specs=pl.BlockSpec((CHIPS, 2, ROWS, BLK), lambda i, order: (0, 0, 0, 0)),
            scratch_shapes=[pltpu.VMEM((2, CHIPS, ROWS, BLK), BF16)],
        ),
        out_shape=jax.ShapeDtypeStruct((CHIPS, 2, ROWS, BLK), BF16),
        compiler_params=params(),
        name="project",
    )(order, *row_sets, own, other)


def unit_sum_kernel(parts_ref, out_ref):
    total = parts_ref[0].astype(F32)
    for index in range(1, CHIPS):
        total = total + parts_ref[index].astype(F32)
    out_ref[...] = total.astype(BF16)


def unit_sum(parts):
    return pl.pallas_call(
        unit_sum_kernel,
        out_shape=jax.ShapeDtypeStruct((2, ROWS, BLK), BF16),
        compiler_params=params(),
        name="unit_sum",
    )(parts)


def finish_kernel(state_ref, attention_ref, mixed_ref, out_ref):
    for half in range(2):
        cols = slice(half * BLK, (half + 1) * BLK)
        out_ref[:, cols] = (
            state_ref[:, cols].astype(F32) + attention_ref[:, cols] + mixed_ref[half].astype(F32)
        ).astype(BF16)


def finish(state, attention, mixed):
    return pl.pallas_call(
        finish_kernel,
        out_shape=jax.ShapeDtypeStruct(state.shape, BF16),
        compiler_params=params(),
        name="finish",
    )(state, attention, mixed)


KEYS = ROWS * SLOTS
FRESH = 2 * STEPS * ROWS
SCALES_AT = 2 * KEYS + FRESH
CACHE_ROWS = SCALES_AT + 16


def pack_kernel(place_ref, keys_ref, values_ref, scale_ref, fresh_ref, out_ref):
    out_ref[:KEYS] = keys_ref[...]
    out_ref[KEYS : 2 * KEYS] = values_ref[...]
    width = fresh_ref.shape[1]
    wide = jnp.concatenate([fresh_ref[...].astype(F32)] * (HD // width), axis=1)
    lane = lax.broadcasted_iota(jnp.int32, wide.shape, 1)
    out_ref[2 * KEYS : SCALES_AT] = jnp.where(lane // width == place_ref[0], wide, 0.0).astype(BF16)
    spread = lax.broadcasted_iota(jnp.int32, (ROWS, KEYS), 1) // SLOTS
    spread = (spread == lax.broadcasted_iota(jnp.int32, (ROWS, KEYS), 0)).astype(BF16)
    lines = jnp.dot(scale_ref[...], spread, preferred_element_type=F32)
    slot = lax.broadcasted_iota(jnp.int32, lines.shape, 0) & (SLOTS - 1)
    lane = lax.broadcasted_iota(jnp.int32, lines.shape, 1) & (SLOTS - 1)
    lines = jnp.where(slot == lane, lines, 0.0)
    rows = [
        jnp.sum(lines[k * SLOTS : (k + 1) * SLOTS, i * HD : (i + 1) * HD], axis=0, keepdims=True)
        for k in range(2)
        for i in range(KEYS // HD)
    ]
    out_ref[SCALES_AT:] = jnp.concatenate(
        rows + [jnp.zeros((16 - len(rows), HD), F32)], axis=0
    ).astype(BF16)


def pack_caches(cache_k, cache_v, cache_scale, fresh_kv, place):
    vmem = pl.BlockSpec(memory_space=pltpu.VMEM)
    return pl.pallas_call(
        pack_kernel,
        in_specs=[pl.BlockSpec(memory_space=pltpu.SMEM)] + [vmem] * 4,
        out_specs=vmem,
        out_shape=jax.ShapeDtypeStruct((CACHE_ROWS, HD), BF16),
        compiler_params=params(),
        name="pack_caches",
    )(
        place[None],
        cache_k.reshape(KEYS, HD),
        cache_v.reshape(KEYS, HD),
        cache_scale.transpose(1, 2, 0).reshape(2 * SLOTS, ROWS),
        fresh_kv.reshape(FRESH, fresh_kv.shape[3]),
    )


def attend_kernel(place_ref, lengths_ref, queries_ref, *refs):
    packed_refs, out_ref = refs[:QUADS], refs[QUADS]
    inv = 1.0 / math.sqrt(HD)
    slots = QUADS * KEYS
    keys = jnp.concatenate([ref[:KEYS] for ref in packed_refs], axis=0)
    values = jnp.concatenate([ref[KEYS : 2 * KEYS] for ref in packed_refs], axis=0)
    fresh = packed_refs[0][2 * KEYS : SCALES_AT].astype(F32)
    for ref in packed_refs[1:]:
        fresh = fresh + ref[2 * KEYS : SCALES_AT].astype(F32)
    new_keys = fresh.astype(BF16)
    new_values = pltpu.roll(fresh, FRESH - 1, 0).astype(BF16)
    scales = [ref[SCALES_AT:].astype(F32) for ref in packed_refs]
    lines = KEYS // HD
    key_scale = jnp.concatenate(
        [scales[p][i : i + 1] for p in range(QUADS) for i in range(lines)], axis=1
    )
    value_scale = jnp.concatenate(
        [scales[p][lines + i : lines + i + 1] for p in range(QUADS) for i in range(lines)], axis=1
    )
    row = lax.broadcasted_iota(jnp.int32, (ROWS, ROWS), 0)
    column = lax.broadcasted_iota(jnp.int32, (ROWS, ROWS), 1)
    length = jnp.where(row == column, lengths_ref[...].astype(F32), 0.0)
    length = jnp.sum(length, axis=1, keepdims=True).astype(jnp.int32)
    lane = lax.broadcasted_iota(jnp.int32, (ROWS, slots), 1)
    row = lax.broadcasted_iota(jnp.int32, (ROWS, slots), 0)
    slot = ((lane // KEYS) ^ place_ref[0]) * SLOTS + (lane & (SLOTS - 1))
    live = ((lane // SLOTS) & (ROWS - 1)) == row
    live = live & (slot < length)
    ahead = slot - length
    window = CACHE - SINK
    lane = lax.broadcasted_iota(jnp.int32, (ROWS, FRESH), 1)
    row = lax.broadcasted_iota(jnp.int32, (ROWS, FRESH), 0)
    mine = (((lane // 2) & (ROWS - 1)) == row) & ((lane & 1) == 0)
    old_sum = [jnp.zeros((ROWS, slots), F32) for _ in range(2)]
    new_sum = [jnp.zeros((ROWS, FRESH), F32) for _ in range(2)]
    for step in range(STEPS):
        evicted = ahead == step
        for turn in range(1, (4 * CACHE + STEPS) // window + 1):
            evicted = evicted | (ahead == step - turn * window)
        live = live & jnp.logical_not(evicted & (slot >= SINK))
        seen = mine & (lane // (2 * ROWS) <= step)
        for head in range(2):
            query = queries_ref[step, :, head * HD : (head + 1) * HD]
            across = (((1,), (1,)), ((), ()))
            old = lax.dot_general(query, keys, across, preferred_element_type=F32)
            old = jnp.where(live, old * (key_scale * inv), -jnp.inf)
            new = lax.dot_general(query, new_keys, across, preferred_element_type=F32) * inv
            new = jnp.where(seen, new, -jnp.inf)
            top = jnp.maximum(
                jnp.max(old, axis=1, keepdims=True), jnp.max(new, axis=1, keepdims=True)
            )
            old = jnp.exp(old - top)
            new = jnp.exp(new - top)
            share = 1.0 / (jnp.sum(old, axis=1, keepdims=True) + jnp.sum(new, axis=1, keepdims=True))
            old_sum[head] = old_sum[head] + old * share
            new_sum[head] = new_sum[head] + new * share
    for head in range(2):
        old = (old_sum[head] * value_scale).astype(BF16)
        new = new_sum[head].astype(BF16)
        out_ref[:, head * HD : (head + 1) * HD] = jnp.dot(
            old, values, preferred_element_type=F32
        ) + jnp.dot(new, new_values, preferred_element_type=F32)


def attend(place, lengths, queries, packed):
    vmem = pl.BlockSpec(memory_space=pltpu.VMEM)
    return pl.pallas_call(
        attend_kernel,
        in_specs=[pl.BlockSpec(memory_space=pltpu.SMEM)] + [vmem] * (2 + QUADS),
        out_specs=vmem,
        out_shape=jax.ShapeDtypeStruct((ROWS, 2 * HD), F32),
        compiler_params=params(),
        name="attend",
    )(place[None], lengths[None], queries, *packed)


def shards(
    grad_partials,
    master,
    moment,
    second,
    state,
    hidden,
    queries,
    fresh_kv,
    cache_k,
    cache_v,
    cache_scale,
    lengths,
):
    dp = lax.axis_index("dp")
    tp = lax.axis_index("tp")
    core, low = dp % 2, dp // 2
    plane = lax.axis_index("grp") * 4 + low
    grad = grad_partials[0]

    outgoing = take_chunks(dp, grad)
    received = flip(outgoing, 1)
    keep, send, units = core_sum(dp, grad, received, hidden)
    second_in = flip(send, 2)

    same = lax.all_to_all(units, "grp", 0, 0)

    third = pair_sum(keep, second_in)
    third_in = flip(third, 4)
    same, _ = lax.optimization_barrier((same, third))
    place = tp % QUADS
    caches = pack_caches(cache_k, cache_v, cache_scale, fresh_kv, place)
    caches, _, _ = lax.optimization_barrier((caches, third, same))
    first = swap(caches, 1)
    two = from_plane(same, lambda plane: 2 if plane % 2 == 0 else -2)
    up = from_plane(same, lambda plane: 1)
    down = from_plane(same, lambda plane: -1)

    codes, own = update(keep, second_in, third_in, master, moment, second)
    own, two, up, down, first = lax.optimization_barrier((own, two, up, down, first))
    other = flip(own, 1)

    row_at = lax.dynamic_index_in_dim(jnp.array(ROW_AT), plane, 0, keepdims=False)
    order = ((row_at - low) & 3) * 4 + row_at // 4
    order = jnp.concatenate([order, core[None]]).astype(jnp.int32)
    parts = project(order, (same, up, two, down), own, other)
    caches, parts = lax.optimization_barrier((caches, parts))
    packed = [caches, first] + [swap(caches, mask) for mask in range(2, QUADS)]
    attention = attend(place, lengths, queries, packed)
    parts = lax.all_to_all(parts, "tp", 0, 0)
    mixed = lax.ppermute(unit_sum(parts), ALL, home_pairs())
    return (codes, finish(state, attention, mixed))


def solution(mesh):
    return jax.shard_map(
        shards,
        mesh=mesh,
        in_specs=(
            P("dp", "tp", "grp"),
            P("tp", ("grp", "dp")),
            P("tp", ("grp", "dp")),
            P("tp", ("grp", "dp")),
            P(("grp", "dp"), "tp"),
            P(None, ("grp", "dp"), "tp"),
            P(None, ("grp", "dp"), "tp"),
            P(None, ("grp", "dp"), None, "tp"),
            P(("grp", "dp"), "tp", None),
            P(("grp", "dp"), "tp", None),
            P(("grp", "dp"), None, "tp"),
            P(("grp", "dp")),
        ),
        out_specs=(P("tp", ("grp", "dp")), P(("grp", "dp"), "tp")),
        check_vma=False,
    )
```
